128 devices in a mesh: section: 2 (over core), tensor: 4 (over x), pool: 16 (over z, y).
Axes of the slice: x: 4, y: 4, z: 4, core: 2. Of those that a mesh axis runs over, the one named last changes fastest.
Arguments:
- hidden_input: bfloat16 [2, 512, 8192], P('section', None, 'pool'), may hold values from -6 to 6
- fresh: bfloat16 [512, 8192], P(None, 'pool'), may hold values from -6 to 6
- gain: float32 [2, 8192], P('section', 'pool'), may hold values from 0.5 to 1.5
- query_matrix: bfloat16 [2, 8192, 8192], P('section', 'pool', 'tensor'), may hold values from -0.0625 to 0.0625
- keyval_matrix: bfloat16 [2, 8192, 2, 1024], P('section', 'pool', None, 'tensor'), may hold values from -0.0625 to 0.0625
- output_weight: bfloat16 [2, 8192, 8192], P('section', 'tensor', 'pool'), may hold values from -0.0625 to 0.0625
- cache: bfloat16 [2, 2, 512, 128, 2, 1024], P('section', None, 'pool', None, None, 'tensor'), may hold values from -6 to 6
- lengths: int32 [3, 512], replicated, may hold values from 1 to 128, as said below
- adapter_of_row: int32 [3, 512], replicated, may hold values from 0 to 31
- adapters_per_batch: int32 [3, 32], replicated, may hold values from 0 to 255, as said below
- adapter_slot_table: int32 [256], replicated, may hold values from 0 to 255, as said below
- adapter_down: bfloat16 [256, 2, 16, 8192], P(('section', 'pool'), None, None, 'tensor'), may hold values from -0.0625 to 0.0625
- adapter_up: bfloat16 [256, 2, 16, 8192], P(('section', 'tensor'), None, None, 'pool'), may hold values from -1.5 to 1.5
Outputs:
- first_tick: bfloat16 [2, 512, 8192], P('section', 'tensor', 'pool')
- second_tick: bfloat16 [2, 512, 8192], P('section', 'tensor', 'pool')
The draws below stay inside these ranges and needn't reach their ends.
Inputs may be any that keep to these rules, and one draw needn't show every extreme that they name: A permutation: adapter a's panels are row adapter_slot_table[a] of adapter_down and of adapter_up. `adapters_per_batch`: adapter numbers; the 32 adapters of a micro-batch have their slots in 32 different blocks of 8 consecutive slots. `lengths`: the first row of every micro-batch has 128 cached positions.
All inputs are finite; a program needn't handle non-finite values.
Results may differ from the reference program's by a relative error of at most 0.012.
Values may be sent and summed in bfloat16 or wider, within the bound.
A program may use at most 128 MiB of HBM per device.

```python
import math
import jax
import jax.numpy as jnp
import numpy as np
from jax import lax

HIDDEN_WIDTH = 8192
QUERY_HEADS = 64
KV_HEADS = 8
HEAD_WIDTH = 128
ADAPTER_RANK = 16
CTX = 128
ROWS = 512
LAYER_COUNT = 2
BATCHES = 3
ACTIVE_ADAPTERS = 32
ADAPTER_POOL = 256


def adapter_slots(key):
    return jax.random.permutation(key, ADAPTER_POOL).astype(jnp.int32)


def draw_adapter_slot_table(key, part):
    slot_of = adapter_slots(key)
    return slot_of


def draw_adapters_per_batch(key, part):
    slot_of = adapter_slots(key)
    key = jax.random.fold_in(key, 7)
    holder = jnp.argsort(slot_of).astype(jnp.int32)
    block_size = ADAPTER_POOL // ACTIVE_ADAPTERS
    positions = jnp.arange(ACTIVE_ADAPTERS, dtype=jnp.int32)
    offsets = jax.random.randint(jax.random.fold_in(key, 1), (BATCHES, ACTIVE_ADAPTERS), 0, 1 << 20, dtype=jnp.int32) % block_size
    chosen = positions[None, :] * block_size + offsets
    first_slot = slot_of[0]
    last_slot = slot_of[ADAPTER_POOL - 1]
    chosen = chosen.at[0, first_slot // block_size].set(first_slot)
    chosen = chosen.at[1, last_slot // block_size].set(last_slot)
    shuffle_keys = jax.random.randint(jax.random.fold_in(key, 2), (BATCHES, ACTIVE_ADAPTERS), 0, 1 << 16, dtype=jnp.int32) * ACTIVE_ADAPTERS + positions[None, :]
    shuffle = jnp.argsort(shuffle_keys, axis=1)
    chosen = jnp.take_along_axis(chosen, shuffle, axis=1)
    return holder[chosen].astype(jnp.int32)


def draw_lengths(key, part):
    key = jax.random.fold_in(key, 11)
    drawn = jax.random.randint(key, (BATCHES, ROWS), 1, CTX + 1, dtype=jnp.int32)
    return drawn.at[:, 0].set(CTX).astype(jnp.int32)


def plant(entries, key, least, largest):
    dims = entries.shape
    place = [jax.random.randint(jax.random.fold_in(key, axis), (), 0, dims[axis]) for axis in range(len(dims))]
    entries = entries.at[tuple(place)].set(least)
    longest = dims.index(max(dims))
    place[longest] = (place[longest] + 1) % dims[longest]
    return entries.at[tuple(place)].set(largest)


def level_of(stream_key, shape, pieces, least, top_value):
    level, own = 1.0, jax.random.fold_in(stream_key, 6)
    for dim, shards_of in pieces:
        draws = jnp.exp(jax.random.uniform(jax.random.fold_in(own, dim), (shards_of,), jnp.float32, least / len(pieces), top_value / len(pieces)))
        level = level * jnp.repeat(draws, shape[dim] // shards_of).reshape([-1 if axis == dim else 1 for axis in range(len(shape))])
    return level


def rank_table(count, skew):
    weights = [(1 << 20) // math.isqrt(rank ** skew) + 1 for rank in range(1, count + 1)]
    spread = 1 + sum(weights) // (1 << 30)
    return np.cumsum(np.array([max(1, weight // spread) for weight in weights]))


def ranked(rng, shape, number_of, skew):
    table = rank_table(number_of, skew)
    pick = jax.random.randint(jax.random.fold_in(rng, 1), shape, 0, int(table[number_of - 1]))
    grade = jnp.searchsorted(jnp.asarray(table, jnp.int32), pick, side="right")
    return jax.random.permutation(jax.random.fold_in(rng, 2), number_of)[grade].astype(jnp.int32)


def normal_values(stream_key, extent, deviation, bound, split=(), held_as=jnp.bfloat16):
    array = jax.random.normal(stream_key, extent, jnp.float32) * deviation
    if len(split) > 0:
        array = level_of(stream_key, extent, split, -0.22, 0.18) * array
    return jnp.clip(array, min=-bound, max=bound).astype(held_as)


def setup_inputs(seed: int = 0) -> dict:
    splits = jax.random.split(jax.random.key(seed), 14)
    hidden_input = normal_values(splits[0], (LAYER_COUNT, ROWS, HIDDEN_WIDTH), 1.0, 6.0, ((0, 2), (2, 16)))
    fresh = normal_values(splits[1], (ROWS, HIDDEN_WIDTH), 1.0, 6.0, ((1, 16),))
    gain = jnp.clip(1.0 + 0.1 * jax.random.normal(splits[2], (LAYER_COUNT, HIDDEN_WIDTH), jnp.float32), 0.5, 1.5)
    query_matrix = normal_values(splits[3], (LAYER_COUNT, HIDDEN_WIDTH, QUERY_HEADS * HEAD_WIDTH), HIDDEN_WIDTH ** -0.5, 0.0625, ((0, 2), (1, 16), (2, 4)))
    keyval_matrix = normal_values(splits[4], (LAYER_COUNT, HIDDEN_WIDTH, 2, KV_HEADS * HEAD_WIDTH), HIDDEN_WIDTH ** -0.5, 0.0625, ((0, 2), (1, 16), (3, 4)))
    output_weight = normal_values(splits[5], (LAYER_COUNT, QUERY_HEADS * HEAD_WIDTH, HIDDEN_WIDTH), (QUERY_HEADS * HEAD_WIDTH) ** -0.5, 0.0625, ((0, 2), (1, 4), (2, 16)))
    cache = normal_values(splits[6], (LAYER_COUNT, 2, ROWS, CTX, 2, KV_HEADS * HEAD_WIDTH), 1.0, 6.0, ((0, 2), (2, 16), (5, 4)))
    lengths = draw_lengths(jax.random.fold_in(splits[13], 71), 0)
    adapter_of_row = plant(ranked(splits[8], (BATCHES, ROWS), ACTIVE_ADAPTERS, 2), jax.random.fold_in(splits[8], 3), 0, ACTIVE_ADAPTERS - 1).astype(jnp.int32)
    adapters_per_batch = draw_adapters_per_batch(jax.random.fold_in(splits[13], 71), 0)
    adapter_slot_table = draw_adapter_slot_table(jax.random.fold_in(splits[13], 71), 0)
    adapter_down = normal_values(splits[11], (ADAPTER_POOL, LAYER_COUNT, ADAPTER_RANK, QUERY_HEADS * HEAD_WIDTH), (QUERY_HEADS * HEAD_WIDTH) ** -0.5, 0.0625, ((0, 32), (3, 4)))
    adapter_up = normal_values(splits[12], (ADAPTER_POOL, LAYER_COUNT, ADAPTER_RANK, HIDDEN_WIDTH), ADAPTER_RANK ** -0.5, 1.5, ((0, 8), (3, 16)))
    return dict(hidden_input=hidden_input, fresh=fresh, gain=gain, query_matrix=query_matrix, keyval_matrix=keyval_matrix, output_weight=output_weight, cache=cache, lengths=lengths, adapter_of_row=adapter_of_row, adapters_per_batch=adapters_per_batch, adapter_slot_table=adapter_slot_table, adapter_down=adapter_down, adapter_up=adapter_up)


NORM_EPS = 1e-05
ADAPTER_SCALE = 2.0
BEST_PRECISION = lax.Precision.HIGHEST

def attend_exact(queries, keyvals, cache_tick, own_lengths):
    row_count = queries.shape[0]
    kv_width = keyvals.shape[2]
    kv_count = kv_width // HEAD_WIDTH
    group_size = queries.shape[1] // kv_width
    context = cache_tick.shape[1]
    query_heads = queries.astype(jnp.float32).reshape(row_count, kv_count, group_size, HEAD_WIDTH)
    key_rows = cache_tick[:, :, 0, :].astype(jnp.float32).reshape(row_count, context, kv_count, HEAD_WIDTH)
    value_rows = cache_tick[:, :, 1, :].astype(jnp.float32).reshape(row_count, context, kv_count, HEAD_WIDTH)
    new_key = keyvals[:, 0, :].astype(jnp.float32).reshape(row_count, kv_count, HEAD_WIDTH)
    new_value = keyvals[:, 1, :].astype(jnp.float32).reshape(row_count, kv_count, HEAD_WIDTH)
    inv_scale = 1.0 / math.sqrt(HEAD_WIDTH)
    scores = jnp.einsum('rkgd,rlkd->rkgl', query_heads, key_rows, precision=BEST_PRECISION) * inv_scale
    own_score = jnp.einsum('rkgd,rkd->rkg', query_heads, new_key, precision=BEST_PRECISION) * inv_scale
    live_mask = jnp.arange(context, dtype=jnp.int32)[None, :] < own_lengths[:, None]
    weights = jnp.where(live_mask[:, None, None, :], jnp.exp(scores), 0.0)
    own_weight = jnp.exp(own_score)
    denominator = lax.optimization_barrier(jnp.sum(weights, axis=3)) + own_weight
    weights_bf = weights.astype(jnp.bfloat16).astype(jnp.float32)
    own_bf = own_weight.astype(jnp.bfloat16).astype(jnp.float32)
    numerator = jnp.einsum('rkgl,rlkd->rkgd', weights_bf, value_rows, precision=BEST_PRECISION)
    numerator = numerator + jnp.einsum('rkg,rkd->rkgd', own_bf, new_value, precision=BEST_PRECISION)
    return (numerator / denominator[..., None]).astype(jnp.bfloat16).reshape(row_count, -1)

def reference(hidden_input, fresh, gain, query_matrix, keyval_matrix, output_weight, cache, lengths, adapter_of_row, adapters_per_batch, adapter_slot_table, adapter_down, adapter_up):

    def layer(hidden, segment_number, batch_num, tick_num):
        expanded_rows = hidden.astype(jnp.float32)
        mean_square = lax.optimization_barrier(jnp.mean(expanded_rows * expanded_rows, axis=1, keepdims=True))
        normed = (expanded_rows * lax.rsqrt(mean_square + NORM_EPS) * gain[segment_number][None, :]).astype(jnp.bfloat16)
        queries = jnp.dot(normed, query_matrix[segment_number], preferred_element_type=jnp.float32).astype(jnp.bfloat16)
        keyvals = jnp.einsum('rd,dke->rke', normed.astype(jnp.float32), keyval_matrix[segment_number].astype(jnp.float32), precision=BEST_PRECISION).astype(jnp.bfloat16)
        attended = attend_exact(queries, keyvals, cache[segment_number, tick_num], lengths[batch_num])
        output_share = jnp.dot(attended, output_weight[segment_number], preferred_element_type=jnp.float32)
        rows_by_slot = adapter_slot_table[adapters_per_batch[batch_num]]
        down_matrices = adapter_down[rows_by_slot, segment_number].astype(jnp.float32)
        up_matrices = adapter_up[rows_by_slot, segment_number].astype(jnp.float32).reshape(ACTIVE_ADAPTERS * ADAPTER_RANK, HIDDEN_WIDTH)
        down_part = jnp.einsum('nq,arq->nar', attended.astype(jnp.float32), down_matrices, precision=BEST_PRECISION)
        chosen = adapter_of_row[batch_num][:, None] == jnp.arange(ACTIVE_ADAPTERS, dtype=jnp.int32)[None, :]
        low_rank = jnp.where(chosen[:, :, None], down_part, 0.0).reshape(ROWS, ACTIVE_ADAPTERS * ADAPTER_RANK)
        adapter_change = jnp.dot(low_rank, up_matrices, precision=BEST_PRECISION)
        return (expanded_rows + output_share + ADAPTER_SCALE * adapter_change).astype(jnp.bfloat16)
    first_list = [layer(hidden_input[segment_number], segment_number, segment_number + 1, 0) for segment_number in range(LAYER_COUNT)]
    second_list = []
    for segment_number in range(LAYER_COUNT):
        incoming = fresh if segment_number == 0 else first_list[segment_number - 1]
        second_list.append(layer(incoming, segment_number, segment_number, 1))
    return (jnp.stack(first_list), jnp.stack(second_list))
```

```python
import functools
import math

import jax
import jax.numpy as jnp
from jax import lax
from jax.experimental import pallas as pl
from jax.experimental.pallas import tpu as pltpu
from jax.sharding import PartitionSpec as P

NORM_EPS = 1e-05
ADAPTER_SCALE = 2.0
MESH = pl.DeviceIdType.MESH
F32 = jnp.float32
BF16 = jnp.bfloat16

RING = 4
ROWS = 512
FEAT = 512
MODEL = 8192
QCOLS = 2048
KVCOLS = 256
HEADS = 16
HEAD = 128
CTX = 128
CW = QCOLS + 2 * KVCOLS + 128
OWN_ROWS = 32
HALF_ROWS = 16
RANK = 16
N_SEM = 224


def dot(a, b):
    return jnp.dot(a, b, preferred_element_type=F32)


def kernel(
    hidden_hbm,
    fresh_hbm,
    gain_ref,
    wq_hbm,
    wkv_hbm,
    wo_hbm,
    cache_hbm,
    len_ref,
    aor_ref,
    apb_ref,
    table_ref,
    down_hbm,
    up_hbm,
    first_ref,
    second_ref,
    wall,
    kvraw,
    wo,
    dn,
    upv,
    sel,
    upbuf,
    kbuf,
    cbuf,
    fwd1,
    fin1,
    c2,
    fin2,
    agbuf,
    ob,
    finx,
    xin,
    ubuf,
    rslot,
    qs,
    kns,
    vns,
    att,
    lrown,
    lrx,
    lrp,
    ssem,
    rsem,
    lsem,
    psend,
    precv,
    turn,
):
    s = lax.axis_index("section")
    t = lax.axis_index("tensor")
    p = lax.axis_index("pool")
    z = p // RING
    y = p % RING
    o = 1 - s
    outs = (first_ref, second_ref)

    def ring(i, d):
        return lax.rem(i + d + 2 * RING, RING)

    def at_z(j):
        return {"pool": j * RING + y}

    def at_y(j):
        return {"pool": z * RING + j}

    def at_x(j):
        return {"tensor": j}

    started = []
    used = [0]

    def remote(src, dst, dev):
        n = used[0]
        used[0] += 1
        assert n < N_SEM
        return pltpu.make_async_remote_copy(
            src_ref=src,
            dst_ref=dst,
            send_sem=ssem.at[n],
            recv_sem=rsem.at[n],
            device_id=dev,
            device_id_type=MESH,
        )

    def tracked(src, dst, dev):
        c = remote(src, dst, dev)
        started.append(c)
        return c

    def send(src, dst, dev):
        c = tracked(src, dst, dev)
        c.start()
        return c

    kvflat = wkv_hbm.reshape(2 * FEAT, KVCOLS)
    cflat = cache_hbm.reshape(2, OWN_ROWS, 2 * CTX, KVCOLS)
    load_x0 = pltpu.make_async_copy(hidden_hbm.at[0], xin.at[0], lsem.at[0])
    load_kv = pltpu.make_async_copy(kvflat, kvraw, lsem.at[1])
    load_wq = pltpu.make_async_copy(wq_hbm.at[0], wall.at[:, 0:QCOLS], lsem.at[2])
    load_up = pltpu.make_async_copy(up_hbm, upv, lsem.at[3])
    load_dn = pltpu.make_async_copy(down_hbm.at[:, s], dn.at[0], lsem.at[4])
    load_c = [
        pltpu.make_async_copy(cflat.at[k], kbuf.at[k], lsem.at[5 + k]) for k in range(2)
    ]
    load_wo = pltpu.make_async_copy(wo_hbm.at[0], wo.at[:, 0:FEAT], lsem.at[7])
    load_x0.start()
    load_kv.start()
    load_wq.start()
    load_fresh = pltpu.make_async_copy(fresh_hbm, xin.at[1], lsem.at[8])

    barrier = pltpu.get_barrier_semaphore()

    def greet(d, _):
        pl.semaphore_signal(
            barrier, inc=1, device_id={"pool": lax.rem(p + d, 16)}, device_id_type=MESH
        )
        return _

    lax.fori_loop(1, 16, greet, 0)
    for d in range(1, RING):
        pl.semaphore_signal(
            barrier, inc=1, device_id={"tensor": ring(t, d)}, device_id_type=MESH
        )
    for d in range(RING):
        pl.semaphore_signal(
            barrier,
            inc=1,
            device_id={"section": o, "tensor": ring(t, d)},
            device_id_type=MESH,
        )

    load_kv.wait()
    pick_r = lax.broadcasted_iota(jnp.int32, (128, 256), 0)
    pick_c = lax.broadcasted_iota(jnp.int32, (128, 256), 1)
    for b in range(4):
        block = kvraw[b * 256 : (b + 1) * 256, :]
        for n in range(2):
            pick = jnp.where(pick_c == 2 * pick_r + n, 1.0, 0.0).astype(BF16)
            wall[
                b * 128 : (b + 1) * 128,
                QCOLS + n * KVCOLS : QCOLS + (n + 1) * KVCOLS,
            ] = dot(pick, block).astype(BF16)

    def project(k):
        for r in range(RING):
            rows = slice(r * 128, (r + 1) * 128)
            xf = xin[k, rows, :].astype(F32)
            ubuf[rows, :] = (xf * gain_ref[...]).astype(BF16)
            ss = jnp.sum(xf * xf, axis=1, keepdims=True)
            cbuf[k, r, :, :, :, QCOLS + 2 * KVCOLS : CW] = (
                jnp.broadcast_to(ss, (128, 128)).astype(BF16).reshape(4, 2, HALF_ROWS, 128)
            )

        def tile(n, _):
            cols = pl.ds(pl.multiple_of(n * 512, 512), 512)
            part = dot(ubuf[...], wall[:, cols])
            cbuf[k, :, :, :, :, cols] = part.astype(BF16).reshape(4, 4, 2, HALF_ROWS, 512)
            return _

        lax.fori_loop(0, (QCOLS + 2 * KVCOLS) // 512, tile, 0)

    class RingSum:
        def __init__(self, i, dev, src, fwd, fin):
            right, left = ring(i, 1), ring(i, -1)
            self.add0, self.fwd0 = src(right, 0), fwd(0)
            self.add1, self.fwd1 = src(left, 1), fwd(1)
            self.f0 = tracked(src(ring(i, 2), 0), fwd(0), dev(right))
            self.f1 = tracked(src(ring(i, 2), 1), fwd(1), dev(left))
            self.a0 = tracked(src(right, 1), fin(0, 1), dev(right))
            self.a1 = tracked(src(left, 0), fin(1, 0), dev(left))
            self.b0 = tracked(self.add0, fin(0, 0), dev(right))
            self.b1 = tracked(self.add1, fin(1, 1), dev(left))

        def begin(self):
            for c in (self.f0, self.f1, self.a0, self.a1):
                c.start()

        def middle(self):
            self.f0.wait_recv()
            v, w = self.add0, self.fwd0
            v[...] = (v[...].astype(F32) + w[...].astype(F32)).astype(BF16)
            self.b0.start()
            self.f1.wait_recv()
            v, w = self.add1, self.fwd1
            v[...] = (v[...].astype(F32) + w[...].astype(F32)).astype(BF16)
            self.b1.start()

        def end(self):
            for c in (self.a0, self.a1, self.b0, self.b1):
                c.wait_recv()

    class RingGather:
        def __init__(self, i, dev, block):
            right, left = ring(i, 1), ring(i, -1)
            self.r0 = tracked(block(i, 0), block(i, 0), dev(right))
            self.l1 = tracked(block(i, 1), block(i, 1), dev(left))
            self.r1 = tracked(block(i, 1), block(i, 1), dev(right))
            self.l0 = tracked(block(i, 0), block(i, 0), dev(left))
            self.f0 = tracked(block(left, 0), block(left, 0), dev(right))
            self.f1 = tracked(block(right, 1), block(right, 1), dev(left))

        def begin(self):
            for c in (self.r0, self.l1, self.r1, self.l0):
                c.start()

        def middle(self):
            self.r0.wait_recv()
            self.f0.start()
            self.l1.wait_recv()
            self.f1.start()

        def end(self):
            for c in (self.r1, self.l0, self.f0, self.f1):
                c.wait_recv()

    class DirectSum:
        def __init__(self, i, dev, src, fin):
            self.copies = [
                tracked(src(ring(i, d)), fin(d - 1), dev(ring(i, d))) for d in (2, 1, 3)
            ]

        def begin(self):
            for c in self.copies:
                c.start()

        def end(self):
            for c in self.copies:
                c.wait_recv()

    class DirectGather:
        def __init__(self, i, dev, block):
            self.copies = [
                tracked(block(i), block(i), dev(ring(i, d))) for d in (2, 1, 3)
            ]

        def begin(self):
            for c in self.copies:
                c.start()

        def end(self):
            for c in self.copies:
                c.wait_recv()

    def pool_rings(k):
        first = [
            RingSum(
                z,
                at_z,
                lambda j, hf: cbuf.at[k, j, 2 * hf : 2 * hf + 2, 0],
                lambda d: fwd1.at[k, 0, d],
                lambda d, hf: fin1.at[k, 0, d, 2 * hf : 2 * hf + 2],
            ),
            RingSum(
                y,
                at_y,
                lambda j, hf: cbuf.at[k, 2 * hf : 2 * hf + 2, j, 1],
                lambda d: fwd1.at[k, 1, d],
                lambda d, hf: fin1.at[k, 1, d, 2 * hf : 2 * hf + 2],
            ),
        ]
        second = [
            DirectSum(
                (y, z)[h],
                (at_y, at_z)[h],
                lambda j, h=h: c2.at[k, h, j],
                lambda n, h=h: fin2.at[k, h, n],
            )
            for h in range(2)
        ]
        return first, second

    def sum_begin(k):
        for r in rings[k][0]:
            r.begin()

    def sum_middle(k):
        for r in rings[k][0]:
            r.middle()

    def sum_second(k):
        first, second = rings[k]
        for h in range(2):
            first[h].end()
            for b in range(RING):
                mine = cbuf[k, z, b, 0] if h == 0 else cbuf[k, b, y, 1]
                c2[k, h, b] = (
                    mine.astype(F32)
                    + fin1[k, h, 0, b].astype(F32)
                    + fin1[k, h, 1, b].astype(F32)
                ).astype(BF16)
            second[h].begin()

    def sum_end(k):
        for h in range(2):
            rings[k][1][h].end()
            total = c2[k, h, y if h == 0 else z].astype(F32)
            for n in range(3):
                total = total + fin2[k, h, n].astype(F32)
            rstd = lax.rsqrt(total[:, QCOLS + 2 * KVCOLS :] * (1.0 / MODEL) + NORM_EPS)

            def part(n):
                return (total[:, n * HEAD : (n + 1) * HEAD] * rstd).astype(BF16).astype(F32)

            keys = [part(HEADS + g) for g in range(2)]
            values = [part(HEADS + 2 + g) for g in range(2)]
            for n in range(HEADS):
                at = pl.ds(h * HALF_ROWS * HEADS + n, HALF_ROWS, stride=HEADS)
                qs[at, :] = part(n)
                kns[at, :] = keys[n // 8]
                vns[at, :] = values[n // 8]

    inv_scale = 1.0 / math.sqrt(HEAD)
    group = 128 // HEADS
    lane = lax.broadcasted_iota(jnp.int32, (1, 128), 1)
    lane_row = lane // HEADS
    low_heads = lane - lane_row * HEADS < 8
    position = lax.broadcasted_iota(jnp.int32, (2 * CTX, 128), 0)
    even = (position & 1) == 0

    def attention(k):
        for i in range(OWN_ROWS // group):
            at = slice(i * 128, (i + 1) * 128)
            q = qs[at, :]
            own = jnp.exp(jnp.sum(q * kns[at, :], axis=1, keepdims=True) * inv_scale)
            qt = q.T
            wide = jnp.concatenate(
                [jnp.where(low_heads, qt, 0.0), jnp.where(low_heads, 0.0, qt)], axis=0
            )
            length = jnp.zeros((1, 128), jnp.int32)
            scores = jnp.zeros((2 * CTX, 128), F32)
            for r in range(group):
                mine = lane_row == r
                scores = scores + dot(
                    kbuf[k, i * group + r], jnp.where(mine, wide, 0.0).astype(BF16)
                )
                length = jnp.where(
                    mine, len_ref[s + 1 - k, p * OWN_ROWS + i * group + r], length
                )
            live = even & (position < 2 * length)
            weights = jnp.where(live, jnp.exp(jnp.where(live, scores, 0.0) * inv_scale), 0.0)
            weights = pltpu.roll(weights, 1, 0).T
            den = jnp.sum(weights, axis=1, keepdims=True) + own
            weights = weights.astype(BF16)
            nums = []
            for r in range(group):
                pv = dot(weights[r * HEADS : (r + 1) * HEADS], kbuf[k, i * group + r])
                nums += [pv[:8, :HEAD], pv[8:, HEAD:]]
            num = jnp.concatenate(nums, axis=0) + own.astype(BF16).astype(F32) * vns[at, :]
            att[at, :] = num / den
        for h in range(2):
            for n in range(HEADS):
                at = pl.ds(h * HALF_ROWS * HEADS + n, HALF_ROWS, stride=HEADS)
                agbuf[k, z, y, h, :, n * HEAD : (n + 1) * HEAD] = att[at, :].astype(BF16)

    def gather_rings(k):
        first = [
            DirectGather(y, at_y, lambda j: agbuf.at[k, z, j, 0]),
            DirectGather(z, at_z, lambda j: agbuf.at[k, j, y, 1]),
        ]
        second = [
            RingGather(z, at_z, lambda j, hf: agbuf.at[k, j, 2 * hf : 2 * hf + 2, 0]),
            RingGather(y, at_y, lambda j, hf: agbuf.at[k, 2 * hf : 2 * hf + 2, j, 1]),
        ]
        return first, second

    def gather_begin(k):
        for r in gathers[k][0]:
            r.begin()

    def gather_second(k):
        first, second = gathers[k]
        for h in range(2):
            first[h].end()
            second[h].begin()

    def gather_end(k):
        second = gathers[k][1]
        for r in second:
            r.middle()
        for r in second:
            r.end()

    def output_products(k):
        for pair in ((2, 1), (3, 0)):
            chunks = [ring(t, d) for d in pair]
            rows = jnp.concatenate([agbuf[k, j].reshape(128, QCOLS) for j in chunks], axis=0)
            both = dot(rows, wo[...])
            for n, j in enumerate(chunks):
                ob[k, j] = both[n * 128 : (n + 1) * 128, :FEAT].astype(BF16)
                down = both[n * 128 : (n + 1) * 128, FEAT:].T
                ids = rslot[pl.ds(k, 1), pl.ds(pl.multiple_of(j * 128, 128), 128)]
                acc = jnp.zeros((RANK, 128), F32)
                for m in range(16):
                    slot = ((s if m < 8 else o) * 16 + p) * 8 + m % 8
                    acc = acc + jnp.where(
                        ids == slot, down[m * RANK : (m + 1) * RANK, :], 0.0
                    )
                lrown[k, j] = acc
            for d in pair:
                if d > 0:
                    lows[k][d - 1].start()
                    tops[k][d - 1].start()

    def output_low(k):
        total = lrown[k, t]
        for d in range(1, RING):
            lows[k][d - 1].wait_recv()
            total = total + lrx[k, ring(t, -d)]
        lrp[k, p] = total.astype(BF16)

        def give(d, _):
            pltpu.make_async_remote_copy(
                src_ref=lrp.at[k, p],
                dst_ref=lrp.at[k, p],
                send_sem=psend.at[k, d],
                recv_sem=precv.at[k, d],
                device_id={"pool": lax.rem(p + d, 16)},
                device_id_type=MESH,
            ).start()
            return _

        lax.fori_loop(1, 16, give, 0)

    def output_delta(k):
        def take(d, _):
            pltpu.make_async_remote_copy(
                src_ref=lrp.at[k, p],
                dst_ref=lrp.at[k, p],
                send_sem=psend.at[k, d],
                recv_sem=precv.at[k, d],
                device_id={"pool": lax.rem(p + d, 16)},
                device_id_type=MESH,
            ).wait()
            return _

        lax.fori_loop(1, 16, take, 0)
        low_rank = lrp[k, 0].astype(F32)
        for n in range(1, 16):
            low_rank = low_rank + lrp[k, n].astype(F32)
        for c in panels[k]:
            c.wait_recv()
        ids = rslot[pl.ds(k, 1), pl.ds(pl.multiple_of(t * 128, 128), 128)]
        block = lax.shift_right_logical(ids, 3)
        wide = jnp.concatenate(
            [jnp.where(block == b, low_rank, 0.0) for b in range(32)], axis=0
        )
        delta = dot(wide.T.astype(BF16), upbuf[k].reshape(512, FEAT))
        row = pl.ds(pl.multiple_of(t * 128, 128), 128)
        total = (
            xin[k, row, :].astype(F32) + ob[k, t].astype(F32) + ADAPTER_SCALE * delta
        )
        for d in range(1, RING):
            tops[k][d - 1].wait_recv()
            total = total + finx[k, d - 1].astype(F32)
        outs[k][0] = total.astype(BF16)

    def slots_and_offsets():
        ids = [aor_ref[pl.ds(s + 1 - k, 1), :] for k in range(2)]
        first_block = (s * RING + t) * 4

        def step(a, carry):
            rows, offs = carry
            slots = [table_ref[apb_ref[c, a]] for c in range(3)]
            new_offs = []
            for c in range(3):
                block = lax.shift_right_logical(slots[c], 3) - first_block
                new_offs += [
                    jnp.where(block == j, slots[c] & 7, offs[4 * c + j]) for j in range(4)
                ]
            new_rows = []
            for k in range(2):
                slot = jnp.where(s == 0, slots[1 - k], slots[2 - k])
                new_rows.append(jnp.where(ids[k] == a, slot, rows[k]))
            return tuple(new_rows), tuple(new_offs)

        rows, offs = lax.fori_loop(
            0,
            32,
            step,
            ((jnp.zeros((1, ROWS), jnp.int32),) * 2, (jnp.int32(0),) * 12),
        )
        for k in range(2):
            rslot[pl.ds(k, 1), :] = rows[k]
        return offs

    def give_panels(offs):
        got = [[], []]
        mine = s * RING + t
        for w in range(2):
            layer = s if w == 0 else o
            for k in range(2):
                for j in range(4):
                    off = jnp.where(layer == 0, offs[4 * (1 - k) + j], offs[4 * (2 - k) + j])
                    sel[w, k, j * RANK : (j + 1) * RANK, :] = upv[8 * j + off, layer]
                if w == 0:
                    upbuf[k, mine] = sel[w, k]
                for d in range(1 if w == 0 else 0, RING):
                    got[k].append(
                        send(
                            sel.at[w, k],
                            upbuf.at[k, mine],
                            {"section": layer, "tensor": ring(t, d)},
                        )
                    )
        return got

    def spread_down():
        for n in range(2):
            for m in range(QCOLS // 128):
                panel = dn[n, :, :, m * 128 : (m + 1) * 128].reshape(8 * RANK, 128)
                wo[m * 128 : (m + 1) * 128, FEAT + n * 128 : FEAT + (n + 1) * 128] = (
                    panel.astype(F32).T.astype(BF16)
                )

    rings = [pool_rings(k) for k in range(2)]
    gathers = [gather_rings(k) for k in range(2)]
    lows = [
        [
            tracked(lrown.at[k, ring(t, d)], lrx.at[k, t], at_x(ring(t, d)))
            for d in range(1, RING)
        ]
        for k in range(2)
    ]
    tops = [
        [
            tracked(ob.at[k, ring(t, d)], finx.at[k, d - 1], at_x(ring(t, d)))
            for d in range(1, RING)
        ]
        for k in range(2)
    ]

    load_x0.wait()
    load_wq.wait()
    load_up.start()
    load_c[0].start()

    @pl.when(s == 0)
    def _():
        load_fresh.start()

    load_wo.start()
    load_dn.start()
    load_c[1].start()
    project(0)
    pl.semaphore_wait(barrier, 22)
    other_down = send(down_hbm.at[:, o], dn.at[1], {"section": o})

    @pl.when(s == 1)
    def _():
        pl.semaphore_wait(turn, 1)

    sum_begin(0)
    offs = slots_and_offsets()
    sum_middle(0)

    @pl.when(s == 0)
    def _():
        load_fresh.wait()
        project(1)

    sum_second(0)
    load_up.wait()
    panels = give_panels(offs)
    sum_end(0)

    @pl.when(s == 0)
    def _():
        pl.semaphore_signal(turn, inc=1, device_id={"section": o}, device_id_type=MESH)

    load_c[0].wait()
    attention(0)
    gather_begin(0)
    load_dn.wait()
    other_down.wait_recv()
    load_wo.wait()
    spread_down()
    gather_second(0)
    gather_end(0)

    row = pl.ds(pl.multiple_of(t * 128, 128), 128)
    relay = [
        remote(first_ref.at[0], xin.at[1, row], {"section": 1, "tensor": ring(t, d)})
        for d in range(RING)
    ]

    @pl.when(s == 1)
    def _():
        for c in relay:
            c.wait_recv()
        project(1)

    sum_begin(1)
    output_products(0)

    @pl.when(s == 1)
    def _():
        sum_middle(1)

    output_low(0)

    @pl.when(s == 1)
    def _():
        sum_second(1)

    output_delta(0)

    @pl.when(s == 0)
    def _():
        for d in (2, 1, 3, 0):
            relay[d].start()
        sum_middle(1)
        sum_second(1)
        for c in relay:
            c.wait_send()

    sum_end(1)
    load_c[1].wait()
    attention(1)
    gather_begin(1)
    gather_second(1)
    gather_end(1)
    output_products(1)
    output_low(1)
    output_delta(1)
    for c in started:
        c.wait_send()


def hand_over(first_in, second_in, first_out, second_out):
    first_out[...] = first_in[...]
    second_out[...] = second_in[...]


def on_device(*args):
    any_space = pl.BlockSpec(memory_space=pl.ANY)
    vmem = pl.BlockSpec(memory_space=pltpu.VMEM)
    smem = pl.BlockSpec(memory_space=pltpu.SMEM)
    out = jax.ShapeDtypeStruct((1, 128, FEAT), BF16)
    v = pltpu.VMEM
    dma = pltpu.SemaphoreType.DMA
    first, second = pl.pallas_call(
        kernel,
        out_shape=(out, out),
        in_specs=[
            any_space,
            any_space,
            vmem,
            any_space,
            any_space,
            any_space,
            any_space,
            smem,
            vmem,
            smem,
            smem,
            any_space,
            any_space,
        ],
        out_specs=(vmem, vmem),
        scratch_shapes=[
            v((FEAT, QCOLS + 2 * KVCOLS), BF16),
            v((2 * FEAT, KVCOLS), BF16),
            v((QCOLS, FEAT + 16 * RANK), BF16),
            v((2, 8, RANK, QCOLS), BF16),
            v((32, 2, RANK, FEAT), BF16),
            v((2, 2, 4 * RANK, FEAT), BF16),
            v((2, 8, 4 * RANK, FEAT), BF16),
            v((2, OWN_ROWS, 2 * CTX, KVCOLS), BF16),
            v((2, RING, RING, 2, HALF_ROWS, CW), BF16),
            v((2, 2, 2, 2, HALF_ROWS, CW), BF16),
            v((2, 2, 2, RING, HALF_ROWS, CW), BF16),
            v((2, 2, RING, HALF_ROWS, CW), BF16),
            v((2, 2, 3, HALF_ROWS, CW), BF16),
            v((2, RING, RING, 2, HALF_ROWS, QCOLS), BF16),
            v((2, RING, 128, FEAT), BF16),
            v((2, 3, 128, FEAT), BF16),
            v((2, ROWS, FEAT), BF16),
            v((ROWS, FEAT), BF16),
            v((8, ROWS), jnp.int32),
            v((OWN_ROWS * HEADS, HEAD), F32),
            v((OWN_ROWS * HEADS, HEAD), F32),
            v((OWN_ROWS * HEADS, HEAD), F32),
            v((OWN_ROWS * HEADS, HEAD), F32),
            v((2, RING, RANK, 128), F32),
            v((2, RING, RANK, 128), F32),
            v((2, 16, RANK, 128), BF16),
            dma((N_SEM,)),
            dma((N_SEM,)),
            dma((9,)),
            dma((2, 16)),
            dma((2, 16)),
            pltpu.SemaphoreType.REGULAR,
        ],
        compiler_params=pltpu.CompilerParams(
            collective_id=0, has_side_effects=True, vmem_limit_bytes=58 * 2**20
        ),
        cost_estimate=pl.CostEstimate(
            flops=8_000_000_000, bytes_accessed=16_000_000, transcendentals=500_000
        ),
    )(*args)
    return pl.pallas_call(
        hand_over,
        out_shape=(out, out),
        in_specs=[vmem, vmem],
        out_specs=(vmem, vmem),
    )(first, second)


def solution(mesh):
    return jax.shard_map(
        on_device,
        mesh=mesh,
        in_specs=(
            P("section", None, "pool"),
            P(None, "pool"),
            P("section", "pool"),
            P("section", "pool", "tensor"),
            P("section", "pool", None, "tensor"),
            P("section", "tensor", "pool"),
            P("section", None, "pool", None, None, "tensor"),
            P(),
            P(),
            P(),
            P(),
            P(("section", "pool"), None, None, "tensor"),
            P(("section", "tensor"), None, None, "pool"),
        ),
        out_specs=(P("section", "tensor", "pool"), P("section", "tensor", "pool")),
        check_vma=False,
    )
```

```python
import functools
import math

import jax
import jax.numpy as jnp
from jax import lax
from jax.experimental import pallas as pl
from jax.experimental.pallas import tpu as pltpu
from jax.sharding import PartitionSpec as P

NORM_EPS = 1e-05
ADAPTER_SCALE = 2.0
MESH = pl.DeviceIdType.MESH
F32 = jnp.float32
BF16 = jnp.bfloat16

RING = 4
ROWS = 512
FEAT = 512
MODEL = 8192
QCOLS = 2048
KVCOLS = 256
HEADS = 16
HEAD = 128
CTX = 128
CW = QCOLS + 2 * KVCOLS + 128
WIDTHS = (1408, CW - 1408)
STARTS = (0, 1408)
OWN_ROWS = 32
HALF_ROWS = 16
RANK = 16
N_SEM = 224


def dot(a, b):
    return jnp.dot(a, b, preferred_element_type=F32)


def kernel(
    hidden_hbm,
    fresh_hbm,
    gain_ref,
    wq_hbm,
    wkv_hbm,
    wo_hbm,
    cache_hbm,
    len_ref,
    aor_ref,
    apb_ref,
    table_ref,
    down_hbm,
    up_hbm,
    first_ref,
    second_ref,
    wall,
    kvraw,
    wo,
    dn,
    upv,
    sel,
    upbuf,
    kbuf,
    cbuf,
    fwd1,
    fin1,
    c2,
    fin2,
    agbuf,
    ob,
    finx,
    xin,
    ubuf,
    half_slot,
    chunk_slot,
    qs,
    kns,
    vns,
    att,
    lrown,
    lrx,
    lrp,
    ssem,
    rsem,
    lsem,
    psend,
    precv,
    turn,
):
    s = lax.axis_index("section")
    t = lax.axis_index("tensor")
    p = lax.axis_index("pool")
    z = p // RING
    y = p % RING
    o = 1 - s
    outs = (first_ref, second_ref)

    def ring(i, d):
        return lax.rem(i + d + 2 * RING, RING)

    def at_z(j):
        return {"pool": j * RING + y}

    def at_y(j):
        return {"pool": z * RING + j}

    def at_x(j):
        return {"tensor": j}

    started = []
    used = [0]

    def remote(src, dst, dev):
        n = used[0]
        used[0] += 1
        assert n < N_SEM
        return pltpu.make_async_remote_copy(
            src_ref=src,
            dst_ref=dst,
            send_sem=ssem.at[n],
            recv_sem=rsem.at[n],
            device_id=dev,
            device_id_type=MESH,
        )

    def tracked(src, dst, dev):
        c = remote(src, dst, dev)
        started.append(c)
        return c

    def send(src, dst, dev):
        c = tracked(src, dst, dev)
        c.start()
        return c

    kvflat = wkv_hbm.reshape(2 * FEAT, KVCOLS)
    cflat = cache_hbm.reshape(2, OWN_ROWS, 2 * CTX, KVCOLS)
    load_x0 = pltpu.make_async_copy(hidden_hbm.at[0], xin.at[0], lsem.at[0])
    load_kv = pltpu.make_async_copy(kvflat, kvraw, lsem.at[1])
    load_wq = pltpu.make_async_copy(wq_hbm.at[0], wall.at[:, 0:QCOLS], lsem.at[2])
    load_up = pltpu.make_async_copy(up_hbm, upv, lsem.at[3])
    load_dn = pltpu.make_async_copy(down_hbm.at[:, s], dn.at[0], lsem.at[4])
    load_c = [
        pltpu.make_async_copy(cflat.at[k], kbuf.at[k], lsem.at[5 + k]) for k in range(2)
    ]
    load_wo = pltpu.make_async_copy(wo_hbm.at[0], wo.at[:, 0:FEAT], lsem.at[7])
    load_x0.start()
    load_kv.start()
    load_wq.start()
    load_fresh = pltpu.make_async_copy(fresh_hbm, xin.at[1], lsem.at[8])

    barrier = pltpu.get_barrier_semaphore()

    def greet(d, _):
        pl.semaphore_signal(
            barrier, inc=1, device_id={"pool": lax.rem(p + d, 16)}, device_id_type=MESH
        )
        return _

    lax.fori_loop(1, 16, greet, 0)
    for d in range(1, RING):
        pl.semaphore_signal(
            barrier, inc=1, device_id={"tensor": ring(t, d)}, device_id_type=MESH
        )
    for d in range(RING):
        pl.semaphore_signal(
            barrier,
            inc=1,
            device_id={"section": o, "tensor": ring(t, d)},
            device_id_type=MESH,
        )

    load_kv.wait()
    pick_r = lax.broadcasted_iota(jnp.int32, (128, 256), 0)
    pick_c = lax.broadcasted_iota(jnp.int32, (128, 256), 1)
    for b in range(4):
        block = kvraw[b * 256 : (b + 1) * 256, :]
        for n in range(2):
            pick = jnp.where(pick_c == 2 * pick_r + n, 1.0, 0.0).astype(BF16)
            wall[
                b * 128 : (b + 1) * 128,
                QCOLS + n * KVCOLS : QCOLS + (n + 1) * KVCOLS,
            ] = dot(pick, block).astype(BF16)

    def project(k, m):
        base = [q * OWN_ROWS + m * HALF_ROWS for q in range(16)]
        xf = jnp.concatenate([xin[k, b : b + HALF_ROWS, :] for b in base], axis=0).astype(F32)
        ubuf[...] = (xf * gain_ref[...]).astype(BF16)
        ss = jnp.sum(xf * xf, axis=1, keepdims=True)
        cbuf[k, m, :, :, :, QCOLS + 2 * KVCOLS : CW] = (
            jnp.broadcast_to(ss, (256, 128)).astype(BF16).reshape(4, 4, HALF_ROWS, 128)
        )

        def tile(n, _):
            cols = pl.ds(pl.multiple_of(n * 512, 512), 512)
            part = dot(ubuf[...], wall[:, cols])
            cbuf[k, m, :, :, :, cols] = part.astype(BF16).reshape(4, 4, HALF_ROWS, 512)
            return _

        lax.fori_loop(0, (QCOLS + 2 * KVCOLS) // 512, tile, 0)

    class RingSum:
        def __init__(self, i, dev, src, fwd, fin):
            right, left = ring(i, 1), ring(i, -1)
            self.add0, self.fwd0 = src(right, 0), fwd(0)
            self.add1, self.fwd1 = src(left, 1), fwd(1)
            self.f0 = tracked(src(ring(i, 2), 0), fwd(0), dev(right))
            self.f1 = tracked(src(ring(i, 2), 1), fwd(1), dev(left))
            self.a0 = tracked(src(right, 1), fin(0, 1), dev(right))
            self.a1 = tracked(src(left, 0), fin(1, 0), dev(left))
            self.b0 = tracked(self.add0, fin(0, 0), dev(right))
            self.b1 = tracked(self.add1, fin(1, 1), dev(left))
            self.copies = [self.f0, self.f1, self.a0, self.a1, self.b0, self.b1]

        def begin(self):
            for c in (self.f0, self.f1, self.a0, self.a1):
                c.start()

        def middle(self):
            self.f0.wait_recv()
            v, w = self.add0, self.fwd0
            v[...] = (v[...].astype(F32) + w[...].astype(F32)).astype(BF16)
            self.b0.start()
            self.f1.wait_recv()
            v, w = self.add1, self.fwd1
            v[...] = (v[...].astype(F32) + w[...].astype(F32)).astype(BF16)
            self.b1.start()

        def end(self):
            for c in (self.a0, self.a1, self.b0, self.b1):
                c.wait_recv()

    class RingGather:
        def __init__(self, i, dev, block):
            right, left = ring(i, 1), ring(i, -1)
            self.r0 = tracked(block(i, 0), block(i, 0), dev(right))
            self.l1 = tracked(block(i, 1), block(i, 1), dev(left))
            self.r1 = tracked(block(i, 1), block(i, 1), dev(right))
            self.l0 = tracked(block(i, 0), block(i, 0), dev(left))
            self.f0 = tracked(block(left, 0), block(left, 0), dev(right))
            self.f1 = tracked(block(right, 1), block(right, 1), dev(left))
            self.copies = [self.r0, self.l1, self.r1, self.l0, self.f0, self.f1]

        def begin(self):
            for c in (self.r0, self.l1, self.r1, self.l0):
                c.start()

        def middle(self):
            self.r0.wait_recv()
            self.f0.start()
            self.l1.wait_recv()
            self.f1.start()

        def end(self):
            for c in (self.r1, self.l0, self.f0, self.f1):
                c.wait_recv()

    class DirectSum:
        def __init__(self, i, dev, src, fin):
            self.copies = [
                tracked(src(ring(i, d)), fin(d - 1), dev(ring(i, d))) for d in (2, 1, 3)
            ]

        def begin(self):
            for c in self.copies:
                c.start()

        def end(self):
            for c in self.copies:
                c.wait_recv()

    class DirectGather:
        def __init__(self, i, dev, block):
            self.copies = [
                tracked(block(i), block(i), dev(ring(i, d))) for d in (2, 1, 3)
            ]

        def begin(self):
            for c in self.copies:
                c.start()

        def end(self):
            for c in self.copies:
                c.wait_recv()

    def pool_rings(k, m):
        def cols(n):
            return slice(STARTS[n], STARTS[n] + WIDTHS[n])

        def own(n):
            return slice(0, WIDTHS[n])

        first = [
            RingSum(
                z,
                at_z,
                lambda j, hf: cbuf.at[k, m, j, 2 * hf : 2 * hf + 2, :, cols(0)],
                lambda d: fwd1.at[k, m, 0, d, :, :, own(0)],
                lambda d, hf: fin1.at[k, m, 0, d, 2 * hf : 2 * hf + 2, :, own(0)],
            ),
            RingSum(
                y,
                at_y,
                lambda j, hf: cbuf.at[k, m, 2 * hf : 2 * hf + 2, j, :, cols(1)],
                lambda d: fwd1.at[k, m, 1, d, :, :, own(1)],
                lambda d, hf: fin1.at[k, m, 1, d, 2 * hf : 2 * hf + 2, :, own(1)],
            ),
        ]
        second = [
            DirectSum(
                (y, z)[n],
                (at_y, at_z)[n],
                lambda j, n=n: c2.at[k, m, n, j, :, own(n)],
                lambda c, n=n: fin2.at[k, m, n, c, :, own(n)],
            )
            for n in range(2)
        ]
        return first, second

    def sum_begin(k, m):
        for r in rings[k][m][0]:
            r.begin()

    def sum_middle(k, m):
        for r in rings[k][m][0]:
            r.middle()

    def sum_second(k, m):
        first, second = rings[k][m]
        for n in range(2):
            first[n].end()
            cols = slice(STARTS[n], STARTS[n] + WIDTHS[n])
            own = slice(0, WIDTHS[n])
            for b in range(RING):
                mine = cbuf[k, m, z, b, :, cols] if n == 0 else cbuf[k, m, b, y, :, cols]
                c2[k, m, n, b, :, own] = (
                    mine.astype(F32)
                    + fin1[k, m, n, 0, b, :, own].astype(F32)
                    + fin1[k, m, n, 1, b, :, own].astype(F32)
                ).astype(BF16)
            second[n].begin()

    def sum_end(k, m):
        totals = []
        for n in range(2):
            rings[k][m][1][n].end()
            own = slice(0, WIDTHS[n])
            total = c2[k, m, n, y if n == 0 else z, :, own].astype(F32)
            for c in range(3):
                total = total + fin2[k, m, n, c, :, own].astype(F32)
            totals.append(total)
        total = jnp.concatenate(totals, axis=1)
        rstd = lax.rsqrt(total[:, QCOLS + 2 * KVCOLS :] * (1.0 / MODEL) + NORM_EPS)

        def part(n):
            return (total[:, n * HEAD : (n + 1) * HEAD] * rstd).astype(BF16).astype(F32)

        keys = [part(HEADS + g) for g in range(2)]
        values = [part(HEADS + 2 + g) for g in range(2)]
        for n in range(HEADS):
            at = pl.ds(m * HALF_ROWS * HEADS + n, HALF_ROWS, stride=HEADS)
            qs[at, :] = part(n)
            kns[at, :] = keys[n // 8]
            vns[at, :] = values[n // 8]

    inv_scale = 1.0 / math.sqrt(HEAD)
    group = 128 // HEADS
    lane = lax.broadcasted_iota(jnp.int32, (1, 128), 1)
    lane_row = lane // HEADS
    low_heads = lane - lane_row * HEADS < 8
    position = lax.broadcasted_iota(jnp.int32, (2 * CTX, 128), 0)
    even = (position & 1) == 0

    def attention(k, i):
        at = slice(i * 128, (i + 1) * 128)
        q = qs[at, :]
        own = jnp.exp(jnp.sum(q * kns[at, :], axis=1, keepdims=True) * inv_scale)
        qt = q.T
        wide = jnp.concatenate(
            [jnp.where(low_heads, qt, 0.0), jnp.where(low_heads, 0.0, qt)], axis=0
        )
        length = jnp.zeros((1, 128), jnp.int32)
        scores = jnp.zeros((2 * CTX, 128), F32)
        for r in range(group):
            mine = lane_row == r
            scores = scores + dot(
                kbuf[k, i * group + r], jnp.where(mine, wide, 0.0).astype(BF16)
            )
            length = jnp.where(
                mine, len_ref[s + 1 - k, p * OWN_ROWS + i * group + r], length
            )
        live = even & (position < 2 * length)
        weights = jnp.where(live, jnp.exp(jnp.where(live, scores, 0.0) * inv_scale), 0.0)
        weights = pltpu.roll(weights, 1, 0).T
        den = jnp.sum(weights, axis=1, keepdims=True) + own
        weights = weights.astype(BF16)
        nums = []
        for r in range(group):
            pv = dot(weights[r * HEADS : (r + 1) * HEADS], kbuf[k, i * group + r])
            nums += [pv[:8, :HEAD], pv[8:, HEAD:]]
        num = jnp.concatenate(nums, axis=0) + own.astype(BF16).astype(F32) * vns[at, :]
        att[at, :] = num / den

    def attended(k, m):
        for n in range(HEADS):
            at = pl.ds(m * HALF_ROWS * HEADS + n, HALF_ROWS, stride=HEADS)
            agbuf[k, m, z, y, :, n * HEAD : (n + 1) * HEAD] = att[at, :].astype(BF16)

    def gather_rings(k, m):
        low, high = slice(0, QCOLS // 2), slice(QCOLS // 2, QCOLS)
        first = [
            DirectGather(y, at_y, lambda j: agbuf.at[k, m, z, j, :, low]),
            DirectGather(z, at_z, lambda j: agbuf.at[k, m, j, y, :, high]),
        ]
        second = [
            RingGather(
                z, at_z, lambda j, hf: agbuf.at[k, m, j, 2 * hf : 2 * hf + 2, :, low]
            ),
            RingGather(
                y, at_y, lambda j, hf: agbuf.at[k, m, 2 * hf : 2 * hf + 2, j, :, high]
            ),
        ]
        return first, second

    def gather_begin(k, m):
        for r in gathers[k][m][0]:
            r.begin()

    def gather_second(k, m):
        first, second = gathers[k][m]
        for n in range(2):
            first[n].end()
            second[n].begin()

    def gather_middle(k, m):
        for r in gathers[k][m][1]:
            r.middle()

    def gather_end(k, m):
        for r in gathers[k][m][1]:
            r.end()

    def down_product(k, m):
        rows = agbuf[k, m].reshape(256, QCOLS)
        down = dot(rows, wo[:, FEAT:]).T
        ids = half_slot[k, m, 0:1, :]
        acc = jnp.zeros((RANK, 256), F32)
        for n in range(16):
            slot = ((s if n < 8 else o) * 16 + p) * 8 + n % 8
            acc = acc + jnp.where(ids == slot, down[n * RANK : (n + 1) * RANK, :], 0.0)
        for j in range(RING):
            lrown[k, j, :, m * 64 : (m + 1) * 64] = acc[:, j * 64 : (j + 1) * 64]
        if m == 1:
            for c in lows[k]:
                c.start()

    def out_product(k, m):
        rows = agbuf[k, m].reshape(256, QCOLS)
        ob[k, m] = dot(rows, wo[:, :FEAT]).astype(BF16).reshape(4, 4, HALF_ROWS, FEAT)
        for d in (2, 1, 3):
            tops[k][m][d - 1].start()

    def output_low(k):
        total = lrown[k, t]
        for d in range(1, RING):
            lows[k][d - 1].wait_recv()
            total = total + lrx[k, ring(t, -d)]
        lrp[k, p] = total.astype(BF16)

        def give(d, _):
            pltpu.make_async_remote_copy(
                src_ref=lrp.at[k, p],
                dst_ref=lrp.at[k, p],
                send_sem=psend.at[k, d],
                recv_sem=precv.at[k, d],
                device_id={"pool": lax.rem(p + d, 16)},
                device_id_type=MESH,
            ).start()
            return _

        lax.fori_loop(1, 16, give, 0)

    def output_delta(k):
        def take(d, _):
            pltpu.make_async_remote_copy(
                src_ref=lrp.at[k, p],
                dst_ref=lrp.at[k, p],
                send_sem=psend.at[k, d],
                recv_sem=precv.at[k, d],
                device_id={"pool": lax.rem(p + d, 16)},
                device_id_type=MESH,
            ).wait()
            return _

        lax.fori_loop(1, 16, take, 0)
        low_rank = lrp[k, 0].astype(F32)
        for n in range(1, 16):
            low_rank = low_rank + lrp[k, n].astype(F32)
        for c in panels[k]:
            c.wait_recv()
        ids = chunk_slot[k, t, 0:1, :]
        block = lax.shift_right_logical(ids, 3)
        wide = jnp.concatenate(
            [jnp.where(block == b, low_rank, 0.0) for b in range(32)], axis=0
        )
        delta = dot(wide.T.astype(BF16), upbuf[k].reshape(512, FEAT))
        for m in range(2):
            for c in tops[k][m]:
                c.wait_recv()
            for b in range(4):
                at = b * OWN_ROWS + m * HALF_ROWS
                row = pl.ds(pl.multiple_of(t * 128, 128) + at, HALF_ROWS)
                total = xin[k, row, :].astype(F32) + ob[k, m, t, b].astype(F32)
                for d in range(3):
                    total = total + finx[k, m, d, b].astype(F32)
                from_row = m * 64 + b * HALF_ROWS
                outs[k][0, at : at + HALF_ROWS, :] = (
                    total + ADAPTER_SCALE * delta[from_row : from_row + HALF_ROWS]
                ).astype(BF16)

    def slots_and_offsets():
        ids = [aor_ref[pl.ds(s + 1 - k, 1), :] for k in range(2)]
        first_block = (s * RING + t) * 4

        def step(a, carry):
            rows, offs = carry
            slots = [table_ref[apb_ref[c, a]] for c in range(3)]
            new_offs = []
            for c in range(3):
                block = lax.shift_right_logical(slots[c], 3) - first_block
                new_offs += [
                    jnp.where(block == j, slots[c] & 7, offs[4 * c + j]) for j in range(4)
                ]
            new_rows = []
            for k in range(2):
                slot = jnp.where(s == 0, slots[1 - k], slots[2 - k])
                new_rows.append(jnp.where(ids[k] == a, slot, rows[k]))
            return tuple(new_rows), tuple(new_offs)

        rows, offs = lax.fori_loop(
            0,
            32,
            step,
            ((jnp.zeros((1, ROWS), jnp.int32),) * 2, (jnp.int32(0),) * 12),
        )
        for k in range(2):

            def piece(j, b, m):
                at = (j * RING + b) * OWN_ROWS + m * HALF_ROWS
                return rows[k][:, at : at + HALF_ROWS]

            for m in range(2):
                half_slot[k, m, 0:1, :] = jnp.concatenate(
                    [piece(j, b, m) for j in range(RING) for b in range(RING)], axis=1
                )
            for j in range(RING):
                chunk_slot[k, j, 0:1, :] = jnp.concatenate(
                    [piece(j, b, m) for m in range(2) for b in range(RING)], axis=1
                )
        return offs

    panels = [[], []]
    holder = s * RING + t
    for w in range(2):
        for k in range(2):
            for d in range(1 if w == 0 else 0, RING):
                panels[k].append(
                    tracked(
                        sel.at[w, k],
                        upbuf.at[k, holder],
                        {"section": s if w == 0 else o, "tensor": ring(t, d)},
                    )
                )

    def slots_and_panels():
        offs = slots_and_offsets()
        load_up.wait()
        for w in range(2):
            layer = s if w == 0 else o
            for k in range(2):
                for j in range(4):
                    off = jnp.where(layer == 0, offs[4 * (1 - k) + j], offs[4 * (2 - k) + j])
                    sel[w, k, j * RANK : (j + 1) * RANK, :] = upv[8 * j + off, layer]
                if w == 0:
                    upbuf[k, holder] = sel[w, k]
        for k in range(2):
            for c in panels[k]:
                c.start()

    def spread_down():
        for n in range(2):
            for m in range(QCOLS // 128):
                panel = dn[n, :, :, m * 128 : (m + 1) * 128].reshape(8 * RANK, 128)
                wo[m * 128 : (m + 1) * 128, FEAT + n * 128 : FEAT + (n + 1) * 128] = (
                    panel.astype(F32).T.astype(BF16)
                )

    rings = [[pool_rings(k, m) for m in range(2)] for k in range(2)]
    gathers = [[gather_rings(k, m) for m in range(2)] for k in range(2)]
    lows = [
        [
            tracked(lrown.at[k, ring(t, d)], lrx.at[k, t], at_x(ring(t, d)))
            for d in range(1, RING)
        ]
        for k in range(2)
    ]
    tops = [
        [
            [
                tracked(ob.at[k, m, ring(t, d)], finx.at[k, m, d - 1], at_x(ring(t, d)))
                for d in range(1, RING)
            ]
            for m in range(2)
        ]
        for k in range(2)
    ]

    def drain(copies):
        for c in copies:
            c.wait_send()
            started[:] = [other for other in started if other is not c]

    def ring_copies(which):
        return [
            c
            for m in range(2)
            for stage in which[m]
            for r in stage
            for c in r.copies
        ]

    load_x0.wait()
    load_wq.wait()
    load_up.start()
    load_c[0].start()

    @pl.when(s == 0)
    def _():
        load_fresh.start()

    load_wo.start()
    load_dn.start()
    load_c[1].start()
    project(0, 0)
    pl.semaphore_wait(barrier, 22)
    other_down = send(down_hbm.at[:, o], dn.at[1], {"section": o})

    @pl.when(s == 1)
    def _():
        project(0, 1)
        slots_and_panels()
        pl.semaphore_wait(turn, 1)

    sum_begin(0, 0)

    @pl.when(s == 0)
    def _():
        project(0, 1)

    sum_middle(0, 0)
    sum_begin(0, 1)

    @pl.when(s == 0)
    def _():
        slots_and_panels()

    sum_second(0, 0)
    sum_middle(0, 1)
    load_dn.wait()
    other_down.wait_recv()
    load_wo.wait()
    spread_down()
    sum_end(0, 0)
    sum_second(0, 1)

    @pl.when(s == 0)
    def _():
        pl.semaphore_signal(turn, inc=1, device_id={"section": o}, device_id_type=MESH)

    load_c[0].wait()
    attention(0, 0)
    attention(0, 1)
    attended(0, 0)
    gather_begin(0, 0)
    sum_end(0, 1)
    attention(0, 2)
    gather_second(0, 0)
    attention(0, 3)
    attended(0, 1)
    gather_begin(0, 1)
    gather_middle(0, 0)
    gather_second(0, 1)

    @pl.when(s == 0)
    def _():
        load_fresh.wait()
        project(1, 0)

    gather_end(0, 0)
    down_product(0, 0)
    gather_middle(0, 1)
    out_product(0, 0)
    gather_end(0, 1)
    down_product(0, 1)

    row = pl.ds(pl.multiple_of(t * 128, 128), 128)
    relay = [
        remote(first_ref.at[0], xin.at[1, row], {"section": 1, "tensor": ring(t, d)})
        for d in range(RING)
    ]

    @pl.when(s == 1)
    def _():
        for c in relay:
            c.wait_recv()
        project(1, 0)

    sum_begin(1, 0)
    out_product(0, 1)
    output_low(0)

    @pl.when(s == 1)
    def _():
        project(1, 1)
        sum_middle(1, 0)
        sum_begin(1, 1)

    output_delta(0)

    @pl.when(s == 0)
    def _():
        for d in (2, 1, 3, 0):
            relay[d].start()
        project(1, 1)
        sum_middle(1, 0)
        sum_begin(1, 1)
        for c in relay:
            c.wait_send()

    drain(ring_copies(rings[0]))
    sum_second(1, 0)
    sum_middle(1, 1)
    drain(ring_copies(gathers[0]))
    drain([other_down] + lows[0] + tops[0][0] + tops[0][1] + panels[0] + panels[1])
    sum_end(1, 0)
    sum_second(1, 1)
    load_c[1].wait()
    attention(1, 0)
    attention(1, 1)
    attended(1, 0)
    gather_begin(1, 0)
    sum_end(1, 1)
    attention(1, 2)
    gather_second(1, 0)
    attention(1, 3)
    attended(1, 1)
    gather_begin(1, 1)
    gather_middle(1, 0)
    gather_second(1, 1)
    drain(ring_copies(rings[1]))
    gather_end(1, 0)
    down_product(1, 0)
    gather_middle(1, 1)
    out_product(1, 0)
    gather_end(1, 1)
    down_product(1, 1)
    out_product(1, 1)
    output_low(1)
    drain(ring_copies(gathers[1]))
    output_delta(1)
    drain(list(started))


def hand_over(first_in, second_in, first_out, second_out):
    first_out[...] = first_in[...]
    second_out[...] = second_in[...]


def on_device(*args):
    any_space = pl.BlockSpec(memory_space=pl.ANY)
    vmem = pl.BlockSpec(memory_space=pltpu.VMEM)
    smem = pl.BlockSpec(memory_space=pltpu.SMEM)
    out = jax.ShapeDtypeStruct((1, 128, FEAT), BF16)
    v = pltpu.VMEM
    dma = pltpu.SemaphoreType.DMA
    first, second = pl.pallas_call(
        kernel,
        out_shape=(out, out),
        in_specs=[
            any_space,
            any_space,
            vmem,
            any_space,
            any_space,
            any_space,
            any_space,
            smem,
            vmem,
            smem,
            smem,
            any_space,
            any_space,
        ],
        out_specs=(vmem, vmem),
        scratch_shapes=[
            v((FEAT, QCOLS + 2 * KVCOLS), BF16),
            v((2 * FEAT, KVCOLS), BF16),
            v((QCOLS, FEAT + 16 * RANK), BF16),
            v((2, 8, RANK, QCOLS), BF16),
            v((32, 2, RANK, FEAT), BF16),
            v((2, 2, 4 * RANK, FEAT), BF16),
            v((2, 8, 4 * RANK, FEAT), BF16),
            v((2, OWN_ROWS, 2 * CTX, KVCOLS), BF16),
            v((2, 2, RING, RING, HALF_ROWS, CW), BF16),
            v((2, 2, 2, 2, 2, HALF_ROWS, WIDTHS[0]), BF16),
            v((2, 2, 2, 2, RING, HALF_ROWS, WIDTHS[0]), BF16),
            v((2, 2, 2, RING, HALF_ROWS, WIDTHS[0]), BF16),
            v((2, 2, 2, 3, HALF_ROWS, WIDTHS[0]), BF16),
            v((2, 2, RING, RING, HALF_ROWS, QCOLS), BF16),
            v((2, 2, RING, RING, HALF_ROWS, FEAT), BF16),
            v((2, 2, 3, RING, HALF_ROWS, FEAT), BF16),
            v((2, ROWS, FEAT), BF16),
            v((ROWS // 2, FEAT), BF16),
            v((2, 2, 8, 256), jnp.int32),
            v((2, RING, 8, 128), jnp.int32),
            v((OWN_ROWS * HEADS, HEAD), F32),
            v((OWN_ROWS * HEADS, HEAD), F32),
            v((OWN_ROWS * HEADS, HEAD), F32),
            v((OWN_ROWS * HEADS, HEAD), F32),
            v((2, RING, RANK, 128), F32),
            v((2, RING, RANK, 128), F32),
            v((2, 16, RANK, 128), BF16),
            dma((N_SEM,)),
            dma((N_SEM,)),
            dma((9,)),
            dma((2, 16)),
            dma((2, 16)),
            pltpu.SemaphoreType.REGULAR,
        ],
        compiler_params=pltpu.CompilerParams(
            collective_id=0, has_side_effects=True, vmem_limit_bytes=58 * 2**20
        ),
        cost_estimate=pl.CostEstimate(
            flops=8_000_000_000, bytes_accessed=16_000_000, transcendentals=500_000
        ),
    )(*args)
    return pl.pallas_call(
        hand_over,
        out_shape=(out, out),
        in_specs=[vmem, vmem],
        out_specs=(vmem, vmem),
    )(first, second)


def solution(mesh):
    return jax.shard_map(
        on_device,
        mesh=mesh,
        in_specs=(
            P("section", None, "pool"),
            P(None, "pool"),
            P("section", "pool"),
            P("section", "pool", "tensor"),
            P("section", "pool", None, "tensor"),
            P("section", "tensor", "pool"),
            P("section", None, "pool", None, None, "tensor"),
            P(),
            P(),
            P(),
            P(),
            P(("section", "pool"), None, None, "tensor"),
            P(("section", "tensor"), None, None, "pool"),
        ),
        out_specs=(P("section", "tensor", "pool"), P("section", "tensor", "pool")),
        check_vma=False,
    )
```

```python
import functools
import math

import jax
import jax.numpy as jnp
from jax import lax
from jax.experimental import pallas as pl
from jax.experimental.pallas import tpu as pltpu
from jax.sharding import PartitionSpec as P

NORM_EPS = 1e-05
ADAPTER_SCALE = 2.0
MESH = pl.DeviceIdType.MESH
F32 = jnp.float32
BF16 = jnp.bfloat16

RING = 4
ROWS = 512
FEAT = 512
MODEL = 8192
QCOLS = 2048
KVCOLS = 256
HEADS = 16
HEAD = 128
CTX = 128
CW = QCOLS + 2 * KVCOLS + 128
WIDTHS = (1408, CW - 1408)
STARTS = (0, 1408)
OWN_ROWS = 32
HALF_ROWS = 16
RANK = 16
N_SEM = 224


def dot(a, b):
    return jnp.dot(a, b, preferred_element_type=F32)


def kernel(
    hidden_hbm,
    fresh_hbm,
    gain_ref,
    wq_hbm,
    wkv_hbm,
    wo_hbm,
    cache_hbm,
    len_ref,
    aor_ref,
    apb_ref,
    table_ref,
    down_hbm,
    up_hbm,
    first_ref,
    second_ref,
    wall,
    kvraw,
    wo,
    dn,
    upv,
    sel,
    upbuf,
    kbuf,
    cbuf,
    fwd1,
    fin1,
    c2,
    fin2,
    agbuf,
    ob,
    finx,
    xin,
    ubuf,
    half_slot,
    chunk_slot,
    qs,
    kns,
    vns,
    att,
    lrown,
    lrx,
    lrp,
    ssem,
    rsem,
    lsem,
    psend,
    precv,
    turn,
):
    s = lax.axis_index("section")
    t = lax.axis_index("tensor")
    p = lax.axis_index("pool")
    z = p // RING
    y = p % RING
    o = 1 - s
    outs = (first_ref, second_ref)

    def ring(i, d):
        return lax.rem(i + d + 2 * RING, RING)

    def at_z(j):
        return {"pool": j * RING + y}

    def at_y(j):
        return {"pool": z * RING + j}

    def at_x(j):
        return {"tensor": j}

    started = []
    used = [0]

    def remote(src, dst, dev):
        n = used[0]
        used[0] += 1
        assert n < N_SEM
        return pltpu.make_async_remote_copy(
            src_ref=src,
            dst_ref=dst,
            send_sem=ssem.at[n],
            recv_sem=rsem.at[n],
            device_id=dev,
            device_id_type=MESH,
        )

    def tracked(src, dst, dev):
        c = remote(src, dst, dev)
        started.append(c)
        return c

    def send(src, dst, dev):
        c = tracked(src, dst, dev)
        c.start()
        return c

    kvflat = wkv_hbm.reshape(2 * FEAT, KVCOLS)
    cflat = cache_hbm.reshape(2, OWN_ROWS, 2 * CTX, KVCOLS)
    load_x0 = pltpu.make_async_copy(hidden_hbm.at[0], xin.at[0], lsem.at[0])
    load_kv = pltpu.make_async_copy(kvflat, kvraw, lsem.at[1])
    load_wq = pltpu.make_async_copy(wq_hbm.at[0], wall.at[:, 0:QCOLS], lsem.at[2])
    load_up = pltpu.make_async_copy(up_hbm, upv, lsem.at[3])
    load_dn = pltpu.make_async_copy(down_hbm.at[:, s], dn.at[0], lsem.at[4])
    load_c = [
        pltpu.make_async_copy(cflat.at[k], kbuf.at[k], lsem.at[5 + k]) for k in range(2)
    ]
    load_wo = pltpu.make_async_copy(wo_hbm.at[0], wo.at[:, 0:FEAT], lsem.at[7])
    load_x0.start()
    load_kv.start()
    load_wq.start()
    load_fresh = pltpu.make_async_copy(fresh_hbm, xin.at[1], lsem.at[8])

    barrier = pltpu.get_barrier_semaphore()

    def greet(d, _):
        pl.semaphore_signal(
            barrier, inc=1, device_id={"pool": lax.rem(p + d, 16)}, device_id_type=MESH
        )
        return _

    lax.fori_loop(1, 16, greet, 0)
    for d in range(1, RING):
        pl.semaphore_signal(
            barrier, inc=1, device_id={"tensor": ring(t, d)}, device_id_type=MESH
        )
    for d in range(RING):
        pl.semaphore_signal(
            barrier,
            inc=1,
            device_id={"section": o, "tensor": ring(t, d)},
            device_id_type=MESH,
        )

    load_kv.wait()
    pick_r = lax.broadcasted_iota(jnp.int32, (128, 256), 0)
    pick_c = lax.broadcasted_iota(jnp.int32, (128, 256), 1)
    for b in range(4):
        block = kvraw[b * 256 : (b + 1) * 256, :]
        for n in range(2):
            pick = jnp.where(pick_c == 2 * pick_r + n, 1.0, 0.0).astype(BF16)
            wall[
                b * 128 : (b + 1) * 128,
                QCOLS + n * KVCOLS : QCOLS + (n + 1) * KVCOLS,
            ] = dot(pick, block).astype(BF16)

    def project(k, m, begin=False, ready=None):
        base = [q * OWN_ROWS + m * HALF_ROWS for q in range(16)]
        xf = jnp.concatenate([xin[k, b : b + HALF_ROWS, :] for b in base], axis=0).astype(F32)
        ubuf[...] = (xf * gain_ref[...]).astype(BF16)
        ss = jnp.sum(xf * xf, axis=1, keepdims=True)
        cbuf[k, m, :, :, :, QCOLS + 2 * KVCOLS : CW] = (
            jnp.broadcast_to(ss, (256, 128)).astype(BF16).reshape(4, 4, HALF_ROWS, 128)
        )

        def tile(n, _):
            cols = pl.ds(pl.multiple_of(n * 512, 512), 512)
            part = dot(ubuf[...], wall[:, cols])
            cbuf[k, m, :, :, :, cols] = part.astype(BF16).reshape(4, 4, HALF_ROWS, 512)
            return _

        lax.fori_loop(0, 3, tile, 0)
        if ready is not None:
            ready()
        if begin:
            rings[k][m][0][0].begin()
        lax.fori_loop(3, 5, tile, 0)
        if begin:
            rings[k][m][0][1].begin()

    class RingSum:
        def __init__(self, i, dev, src, fwd, fin):
            right, left = ring(i, 1), ring(i, -1)
            self.add0, self.fwd0 = src(right, 0), fwd(0)
            self.add1, self.fwd1 = src(left, 1), fwd(1)
            self.f0 = tracked(src(ring(i, 2), 0), fwd(0), dev(right))
            self.f1 = tracked(src(ring(i, 2), 1), fwd(1), dev(left))
            self.a0 = tracked(src(right, 1), fin(0, 1), dev(right))
            self.a1 = tracked(src(left, 0), fin(1, 0), dev(left))
            self.b0 = tracked(self.add0, fin(0, 0), dev(right))
            self.b1 = tracked(self.add1, fin(1, 1), dev(left))
            self.copies = [self.f0, self.f1, self.a0, self.a1, self.b0, self.b1]

        def begin(self):
            for c in (self.f0, self.f1, self.a0, self.a1):
                c.start()

        def middle(self):
            self.f0.wait_recv()
            v, w = self.add0, self.fwd0
            v[...] = (v[...].astype(F32) + w[...].astype(F32)).astype(BF16)
            self.b0.start()
            self.f1.wait_recv()
            v, w = self.add1, self.fwd1
            v[...] = (v[...].astype(F32) + w[...].astype(F32)).astype(BF16)
            self.b1.start()

        def end(self):
            for c in (self.a0, self.a1, self.b0, self.b1):
                c.wait_recv()

    class RingGather:
        def __init__(self, i, dev, block):
            right, left = ring(i, 1), ring(i, -1)
            self.r0 = tracked(block(i, 0), block(i, 0), dev(right))
            self.l1 = tracked(block(i, 1), block(i, 1), dev(left))
            self.r1 = tracked(block(i, 1), block(i, 1), dev(right))
            self.l0 = tracked(block(i, 0), block(i, 0), dev(left))
            self.f0 = tracked(block(left, 0), block(left, 0), dev(right))
            self.f1 = tracked(block(right, 1), block(right, 1), dev(left))
            self.copies = [self.r0, self.l1, self.r1, self.l0, self.f0, self.f1]

        def begin(self):
            for c in (self.r0, self.l1, self.r1, self.l0):
                c.start()

        def middle(self):
            self.r0.wait_recv()
            self.f0.start()
            self.l1.wait_recv()
            self.f1.start()

        def end(self):
            for c in (self.r1, self.l0, self.f0, self.f1):
                c.wait_recv()

    class DirectSum:
        def __init__(self, i, dev, src, fin):
            self.copies = [
                tracked(src(ring(i, d)), fin(d - 1), dev(ring(i, d))) for d in (2, 1, 3)
            ]

        def begin(self):
            for c in self.copies:
                c.start()

        def end(self):
            for c in self.copies:
                c.wait_recv()

    class DirectGather:
        def __init__(self, i, dev, block):
            self.copies = [
                tracked(block(i), block(i), dev(ring(i, d))) for d in (2, 1, 3)
            ]

        def begin(self):
            for c in self.copies:
                c.start()

        def end(self):
            for c in self.copies:
                c.wait_recv()

    def pool_rings(k, m):
        def cols(n):
            return slice(STARTS[n], STARTS[n] + WIDTHS[n])

        def own(n):
            return slice(0, WIDTHS[n])

        first = [
            RingSum(
                z,
                at_z,
                lambda j, hf: cbuf.at[k, m, j, 2 * hf : 2 * hf + 2, :, cols(0)],
                lambda d: fwd1.at[k, m, 0, d, :, :, own(0)],
                lambda d, hf: fin1.at[k, m, 0, d, 2 * hf : 2 * hf + 2, :, own(0)],
            ),
            RingSum(
                y,
                at_y,
                lambda j, hf: cbuf.at[k, m, 2 * hf : 2 * hf + 2, j, :, cols(1)],
                lambda d: fwd1.at[k, m, 1, d, :, :, own(1)],
                lambda d, hf: fin1.at[k, m, 1, d, 2 * hf : 2 * hf + 2, :, own(1)],
            ),
        ]
        second = [
            DirectSum(
                (y, z)[n],
                (at_y, at_z)[n],
                lambda j, n=n: c2.at[k, m, n, j, :, own(n)],
                lambda c, n=n: fin2.at[k, m, n, c, :, own(n)],
            )
            for n in range(2)
        ]
        return first, second

    def sum_begin(k, m):
        for r in rings[k][m][0]:
            r.begin()

    def sum_middle(k, m):
        for r in rings[k][m][0]:
            r.middle()

    def sum_second(k, m):
        first, second = rings[k][m]
        for n in range(2):
            first[n].end()
            cols = slice(STARTS[n], STARTS[n] + WIDTHS[n])
            own = slice(0, WIDTHS[n])
            for b in range(RING):
                mine = cbuf[k, m, z, b, :, cols] if n == 0 else cbuf[k, m, b, y, :, cols]
                c2[k, m, n, b, :, own] = (
                    mine.astype(F32)
                    + fin1[k, m, n, 0, b, :, own].astype(F32)
                    + fin1[k, m, n, 1, b, :, own].astype(F32)
                ).astype(BF16)
            second[n].begin()

    def sum_end(k, m):
        totals = []
        for n in range(2):
            rings[k][m][1][n].end()
            own = slice(0, WIDTHS[n])
            total = c2[k, m, n, y if n == 0 else z, :, own].astype(F32)
            for c in range(3):
                total = total + fin2[k, m, n, c, :, own].astype(F32)
            totals.append(total)
        total = jnp.concatenate(totals, axis=1)
        rstd = lax.rsqrt(total[:, QCOLS + 2 * KVCOLS :] * (1.0 / MODEL) + NORM_EPS)

        def part(n):
            return (total[:, n * HEAD : (n + 1) * HEAD] * rstd).astype(BF16).astype(F32)

        keys = [part(HEADS + g) for g in range(2)]
        values = [part(HEADS + 2 + g) for g in range(2)]
        for n in range(HEADS):
            at = pl.ds(m * HALF_ROWS * HEADS + n, HALF_ROWS, stride=HEADS)
            qs[at, :] = part(n)
            kns[at, :] = keys[n // 8]
            vns[at, :] = values[n // 8]

    inv_scale = 1.0 / math.sqrt(HEAD)
    group = 128 // HEADS
    lane = lax.broadcasted_iota(jnp.int32, (1, 128), 1)
    lane_row = lane // HEADS
    low_heads = lane - lane_row * HEADS < 8
    position = lax.broadcasted_iota(jnp.int32, (2 * CTX, 128), 0)
    even = (position & 1) == 0

    def attention(k, i):
        at = slice(i * 128, (i + 1) * 128)
        q = qs[at, :]
        own = jnp.exp(jnp.sum(q * kns[at, :], axis=1, keepdims=True) * inv_scale)
        qt = q.T
        wide = jnp.concatenate(
            [jnp.where(low_heads, qt, 0.0), jnp.where(low_heads, 0.0, qt)], axis=0
        )
        length = jnp.zeros((1, 128), jnp.int32)
        scores = jnp.zeros((2 * CTX, 128), F32)
        for r in range(group):
            mine = lane_row == r
            scores = scores + dot(
                kbuf[k, i * group + r], jnp.where(mine, wide, 0.0).astype(BF16)
            )
            length = jnp.where(
                mine, len_ref[s + 1 - k, p * OWN_ROWS + i * group + r], length
            )
        live = even & (position < 2 * length)
        weights = jnp.where(live, jnp.exp(jnp.where(live, scores, 0.0) * inv_scale), 0.0)
        weights = pltpu.roll(weights, 1, 0).T
        den = jnp.sum(weights, axis=1, keepdims=True) + own
        weights = weights.astype(BF16)
        nums = []
        for r in range(group):
            pv = dot(weights[r * HEADS : (r + 1) * HEADS], kbuf[k, i * group + r])
            nums += [pv[:8, :HEAD], pv[8:, HEAD:]]
        num = jnp.concatenate(nums, axis=0) + own.astype(BF16).astype(F32) * vns[at, :]
        att[at, :] = num / den

    def attended(k, m):
        for n in range(HEADS):
            at = pl.ds(m * HALF_ROWS * HEADS + n, HALF_ROWS, stride=HEADS)
            agbuf[k, m, z, y, :, n * HEAD : (n + 1) * HEAD] = att[at, :].astype(BF16)

    def gather_rings(k, m):
        low, high = slice(0, QCOLS // 2), slice(QCOLS // 2, QCOLS)
        first = [
            DirectGather(y, at_y, lambda j: agbuf.at[k, m, z, j, :, low]),
            DirectGather(z, at_z, lambda j: agbuf.at[k, m, j, y, :, high]),
        ]
        second = [
            RingGather(
                z, at_z, lambda j, hf: agbuf.at[k, m, j, 2 * hf : 2 * hf + 2, :, low]
            ),
            RingGather(
                y, at_y, lambda j, hf: agbuf.at[k, m, 2 * hf : 2 * hf + 2, j, :, high]
            ),
        ]
        return first, second

    def gather_begin(k, m):
        for r in gathers[k][m][0]:
            r.begin()

    def gather_second(k, m):
        first, second = gathers[k][m]
        for n in range(2):
            first[n].end()
            second[n].begin()

    def gather_middle(k, m):
        for r in gathers[k][m][1]:
            r.middle()

    def gather_end(k, m):
        for r in gathers[k][m][1]:
            r.end()

    def down_product(k, m):
        rows = agbuf[k, m].reshape(256, QCOLS)
        down = dot(rows, wo[:, FEAT:]).T
        ids = half_slot[k, m, 0:1, :]
        acc = jnp.zeros((RANK, 256), F32)
        for n in range(16):
            slot = ((s if n < 8 else o) * 16 + p) * 8 + n % 8
            acc = acc + jnp.where(ids == slot, down[n * RANK : (n + 1) * RANK, :], 0.0)
        for j in range(RING):
            lrown[k, j, :, m * 64 : (m + 1) * 64] = acc[:, j * 64 : (j + 1) * 64]
        if m == 1:
            for c in lows[k]:
                c.start()

    def out_product(k, m):
        rows = agbuf[k, m].reshape(256, QCOLS)
        ob[k, m] = dot(rows, wo[:, :FEAT]).astype(BF16).reshape(4, 4, HALF_ROWS, FEAT)
        for d in (2, 1, 3):
            tops[k][m][d - 1].start()

    def output_low(k):
        total = lrown[k, t]
        for d in range(1, RING):
            lows[k][d - 1].wait_recv()
            total = total + lrx[k, ring(t, -d)]
        lrp[k, p] = total.astype(BF16)

        def give(d, _):
            pltpu.make_async_remote_copy(
                src_ref=lrp.at[k, p],
                dst_ref=lrp.at[k, p],
                send_sem=psend.at[k, d],
                recv_sem=precv.at[k, d],
                device_id={"pool": lax.rem(p + d, 16)},
                device_id_type=MESH,
            ).start()
            return _

        lax.fori_loop(1, 16, give, 0)

    def output_delta(k):
        def take(d, _):
            pltpu.make_async_remote_copy(
                src_ref=lrp.at[k, p],
                dst_ref=lrp.at[k, p],
                send_sem=psend.at[k, d],
                recv_sem=precv.at[k, d],
                device_id={"pool": lax.rem(p + d, 16)},
                device_id_type=MESH,
            ).wait()
            return _

        lax.fori_loop(1, 16, take, 0)
        low_rank = lrp[k, 0].astype(F32)
        for n in range(1, 16):
            low_rank = low_rank + lrp[k, n].astype(F32)
        for c in panels[k]:
            c.wait_recv()
        ids = chunk_slot[k, t, 0:1, :]
        block = lax.shift_right_logical(ids, 3)
        wide = jnp.concatenate(
            [jnp.where(block == b, low_rank, 0.0) for b in range(32)], axis=0
        )
        delta = dot(wide.T.astype(BF16), upbuf[k].reshape(512, FEAT))
        for m in range(2):
            for c in tops[k][m]:
                c.wait_recv()
            for b in range(4):
                at = b * OWN_ROWS + m * HALF_ROWS
                row = pl.ds(pl.multiple_of(t * 128, 128) + at, HALF_ROWS)
                total = xin[k, row, :].astype(F32) + ob[k, m, t, b].astype(F32)
                for d in range(3):
                    total = total + finx[k, m, d, b].astype(F32)
                from_row = m * 64 + b * HALF_ROWS
                outs[k][0, at : at + HALF_ROWS, :] = (
                    total + ADAPTER_SCALE * delta[from_row : from_row + HALF_ROWS]
                ).astype(BF16)

    def slots_and_offsets():
        ids = [aor_ref[pl.ds(s + 1 - k, 1), :] for k in range(2)]
        first_block = (s * RING + t) * 4

        def step(a, carry):
            rows, offs = carry
            slots = [table_ref[apb_ref[c, a]] for c in range(3)]
            new_offs = []
            for c in range(3):
                block = lax.shift_right_logical(slots[c], 3) - first_block
                new_offs += [
                    jnp.where(block == j, slots[c] & 7, offs[4 * c + j]) for j in range(4)
                ]
            new_rows = []
            for k in range(2):
                slot = jnp.where(s == 0, slots[1 - k], slots[2 - k])
                new_rows.append(jnp.where(ids[k] == a, slot, rows[k]))
            return tuple(new_rows), tuple(new_offs)

        rows, offs = lax.fori_loop(
            0,
            32,
            step,
            ((jnp.zeros((1, ROWS), jnp.int32),) * 2, (jnp.int32(0),) * 12),
        )
        for k in range(2):

            def piece(j, b, m):
                at = (j * RING + b) * OWN_ROWS + m * HALF_ROWS
                return rows[k][:, at : at + HALF_ROWS]

            for m in range(2):
                half_slot[k, m, 0:1, :] = jnp.concatenate(
                    [piece(j, b, m) for j in range(RING) for b in range(RING)], axis=1
                )
            for j in range(RING):
                chunk_slot[k, j, 0:1, :] = jnp.concatenate(
                    [piece(j, b, m) for m in range(2) for b in range(RING)], axis=1
                )
        return offs

    panels = [[], []]
    holder = s * RING + t
    for w in range(2):
        for k in range(2):
            for d in range(1 if w == 0 else 0, RING):
                panels[k].append(
                    tracked(
                        sel.at[w, k],
                        upbuf.at[k, holder],
                        {"section": s if w == 0 else o, "tensor": ring(t, d)},
                    )
                )

    def give_panels(offs):
        load_up.wait()
        for w in range(2):
            layer = s if w == 0 else o
            for k in range(2):
                for j in range(4):
                    off = jnp.where(layer == 0, offs[4 * (1 - k) + j], offs[4 * (2 - k) + j])
                    sel[w, k, j * RANK : (j + 1) * RANK, :] = upv[8 * j + off, layer]
                if w == 0:
                    upbuf[k, holder] = sel[w, k]
        for k in range(2):
            for c in panels[k]:
                c.start()

    def spread_down():
        for n in range(2):
            for m in range(QCOLS // 128):
                panel = dn[n, :, :, m * 128 : (m + 1) * 128].reshape(8 * RANK, 128)
                wo[m * 128 : (m + 1) * 128, FEAT + n * 128 : FEAT + (n + 1) * 128] = (
                    panel.astype(F32).T.astype(BF16)
                )

    rings = [[pool_rings(k, m) for m in range(2)] for k in range(2)]
    gathers = [[gather_rings(k, m) for m in range(2)] for k in range(2)]
    lows = [
        [
            tracked(lrown.at[k, ring(t, d)], lrx.at[k, t], at_x(ring(t, d)))
            for d in range(1, RING)
        ]
        for k in range(2)
    ]
    tops = [
        [
            [
                tracked(ob.at[k, m, ring(t, d)], finx.at[k, m, d - 1], at_x(ring(t, d)))
                for d in range(1, RING)
            ]
            for m in range(2)
        ]
        for k in range(2)
    ]

    def drain(copies):
        for c in copies:
            c.wait_send()
            started[:] = [other for other in started if other is not c]

    def ring_copies(which):
        return [
            c
            for m in range(2)
            for stage in which[m]
            for r in stage
            for c in r.copies
        ]

    load_x0.wait()
    load_wq.wait()
    load_up.start()
    load_c[0].start()

    @pl.when(s == 0)
    def _():
        load_fresh.start()

    load_wo.start()
    load_dn.start()
    load_c[1].start()
    other_down = tracked(down_hbm.at[:, o], dn.at[1], {"section": o})

    def everyone_is_here():
        pl.semaphore_wait(barrier, 22)

    @pl.when(s == 0)
    def _():
        project(0, 0, begin=True, ready=everyone_is_here)
        other_down.start()
        project(0, 1)
        sum_middle(0, 0)
        sum_begin(0, 1)
        offs = slots_and_offsets()
        sum_middle(0, 1)
        sum_second(0, 0)
        give_panels(offs)
        load_fresh.wait()
        project(1, 0)

    @pl.when(s == 1)
    def _():
        project(0, 0)
        everyone_is_here()
        other_down.start()
        project(0, 1)
        give_panels(slots_and_offsets())
        pl.semaphore_wait(turn, 1)
        sum_begin(0, 0)
        sum_middle(0, 0)
        sum_begin(0, 1)
        sum_middle(0, 1)
        sum_second(0, 0)

    sum_end(0, 0)
    sum_second(0, 1)

    @pl.when(s == 0)
    def _():
        pl.semaphore_signal(turn, inc=1, device_id={"section": o}, device_id_type=MESH)

    load_c[0].wait()
    attention(0, 0)
    attention(0, 1)
    attended(0, 0)
    gather_begin(0, 0)
    sum_end(0, 1)
    attention(0, 2)
    gather_second(0, 0)
    attention(0, 3)
    attended(0, 1)
    gather_begin(0, 1)
    gather_middle(0, 0)
    gather_second(0, 1)
    load_dn.wait()
    other_down.wait_recv()
    load_wo.wait()
    spread_down()
    gather_end(0, 0)
    gather_middle(0, 1)
    down_product(0, 0)
    out_product(0, 0)
    gather_end(0, 1)
    down_product(0, 1)

    row = pl.ds(pl.multiple_of(t * 128, 128), 128)
    relay = [
        remote(first_ref.at[0], xin.at[1, row], {"section": 1, "tensor": ring(t, d)})
        for d in range(RING)
    ]

    @pl.when(s == 0)
    def _():
        out_product(0, 1)
        sum_begin(1, 0)
        output_low(0)
        output_delta(0)
        for d in (2, 1, 3, 0):
            relay[d].start()
        project(1, 1)
        sum_middle(1, 0)
        sum_begin(1, 1)
        for c in relay:
            c.wait_send()
        sum_middle(1, 1)
        sum_second(1, 0)

    @pl.when(s == 1)
    def _():
        for c in relay:
            c.wait_recv()
        project(1, 0, begin=True)
        project(1, 1)
        sum_middle(1, 0)
        sum_begin(1, 1)
        out_product(0, 1)
        sum_middle(1, 1)
        sum_second(1, 0)
        output_low(0)

    sum_end(1, 0)
    sum_second(1, 1)
    load_c[1].wait()
    attention(1, 0)
    attention(1, 1)
    attended(1, 0)
    gather_begin(1, 0)
    sum_end(1, 1)
    attention(1, 2)
    gather_second(1, 0)
    attention(1, 3)
    attended(1, 1)
    gather_begin(1, 1)
    gather_middle(1, 0)
    drain(ring_copies(rings[0]))
    gather_second(1, 1)

    @pl.when(s == 1)
    def _():
        output_delta(0)

    gather_end(1, 0)
    gather_middle(1, 1)
    drain(ring_copies(gathers[0]))
    down_product(1, 0)
    out_product(1, 0)
    drain([other_down] + lows[0] + tops[0][0] + tops[0][1] + panels[0] + panels[1])
    gather_end(1, 1)
    down_product(1, 1)
    out_product(1, 1)
    output_low(1)
    drain(ring_copies(rings[1]))
    drain(ring_copies(gathers[1]))
    output_delta(1)
    drain(list(started))


def hand_over(first_in, second_in, first_out, second_out):
    first_out[...] = first_in[...]
    second_out[...] = second_in[...]


def on_device(*args):
    any_space = pl.BlockSpec(memory_space=pl.ANY)
    vmem = pl.BlockSpec(memory_space=pltpu.VMEM)
    smem = pl.BlockSpec(memory_space=pltpu.SMEM)
    out = jax.ShapeDtypeStruct((1, 128, FEAT), BF16)
    v = pltpu.VMEM
    dma = pltpu.SemaphoreType.DMA
    first, second = pl.pallas_call(
        kernel,
        out_shape=(out, out),
        in_specs=[
            any_space,
            any_space,
            vmem,
            any_space,
            any_space,
            any_space,
            any_space,
            smem,
            vmem,
            smem,
            smem,
            any_space,
            any_space,
        ],
        out_specs=(vmem, vmem),
        scratch_shapes=[
            v((FEAT, QCOLS + 2 * KVCOLS), BF16),
            v((2 * FEAT, KVCOLS), BF16),
            v((QCOLS, FEAT + 16 * RANK), BF16),
            v((2, 8, RANK, QCOLS), BF16),
            v((32, 2, RANK, FEAT), BF16),
            v((2, 2, 4 * RANK, FEAT), BF16),
            v((2, 8, 4 * RANK, FEAT), BF16),
            v((2, OWN_ROWS, 2 * CTX, KVCOLS), BF16),
            v((2, 2, RING, RING, HALF_ROWS, CW), BF16),
            v((2, 2, 2, 2, 2, HALF_ROWS, WIDTHS[0]), BF16),
            v((2, 2, 2, 2, RING, HALF_ROWS, WIDTHS[0]), BF16),
            v((2, 2, 2, RING, HALF_ROWS, WIDTHS[0]), BF16),
            v((2, 2, 2, 3, HALF_ROWS, WIDTHS[0]), BF16),
            v((2, 2, RING, RING, HALF_ROWS, QCOLS), BF16),
            v((2, 2, RING, RING, HALF_ROWS, FEAT), BF16),
            v((2, 2, 3, RING, HALF_ROWS, FEAT), BF16),
            v((2, ROWS, FEAT), BF16),
            v((ROWS // 2, FEAT), BF16),
            v((2, 2, 8, 256), jnp.int32),
            v((2, RING, 8, 128), jnp.int32),
            v((OWN_ROWS * HEADS, HEAD), F32),
            v((OWN_ROWS * HEADS, HEAD), F32),
            v((OWN_ROWS * HEADS, HEAD), F32),
            v((OWN_ROWS * HEADS, HEAD), F32),
            v((2, RING, RANK, 128), F32),
            v((2, RING, RANK, 128), F32),
            v((2, 16, RANK, 128), BF16),
            dma((N_SEM,)),
            dma((N_SEM,)),
            dma((9,)),
            dma((2, 16)),
            dma((2, 16)),
            pltpu.SemaphoreType.REGULAR,
        ],
        compiler_params=pltpu.CompilerParams(
            collective_id=0, has_side_effects=True, vmem_limit_bytes=58 * 2**20
        ),
        cost_estimate=pl.CostEstimate(
            flops=8_000_000_000, bytes_accessed=16_000_000, transcendentals=500_000
        ),
    )(*args)
    return pl.pallas_call(
        hand_over,
        out_shape=(out, out),
        in_specs=[vmem, vmem],
        out_specs=(vmem, vmem),
    )(first, second)


def solution(mesh):
    return jax.shard_map(
        on_device,
        mesh=mesh,
        in_specs=(
            P("section", None, "pool"),
            P(None, "pool"),
            P("section", "pool"),
            P("section", "pool", "tensor"),
            P("section", "pool", None, "tensor"),
            P("section", "tensor", "pool"),
            P("section", None, "pool", None, None, "tensor"),
            P(),
            P(),
            P(),
            P(),
            P(("section", "pool"), None, None, "tensor"),
            P(("section", "tensor"), None, None, "pool"),
        ),
        out_specs=(P("section", "tensor", "pool"), P("section", "tensor", "pool")),
        check_vma=False,
    )
```

```python
import functools
import math

import jax
import jax.numpy as jnp
from jax import lax
from jax.experimental import pallas as pl
from jax.experimental.pallas import tpu as pltpu
from jax.sharding import PartitionSpec as P

NORM_EPS = 1e-05
ADAPTER_SCALE = 2.0
MESH = pl.DeviceIdType.MESH
F32 = jnp.float32
BF16 = jnp.bfloat16

RING = 4
ROWS = 512
FEAT = 512
MODEL = 8192
QCOLS = 2048
KVCOLS = 256
HEADS = 16
HEAD = 128
CTX = 128
CW = QCOLS + 2 * KVCOLS + 128
WIDTHS = (1408, CW - 1408)
STARTS = (0, 1408)
OWN_ROWS = 32
HALF_ROWS = 16
RANK = 16
N_SEM = 224


def dot(a, b):
    return jnp.dot(a, b, preferred_element_type=F32)


def kernel(
    hidden_hbm,
    fresh_hbm,
    gain_ref,
    wq_hbm,
    wkv_hbm,
    wo_hbm,
    cache_hbm,
    len_ref,
    aor_ref,
    apb_ref,
    table_ref,
    down_hbm,
    up_hbm,
    first_ref,
    second_ref,
    wall,
    kvraw,
    wo,
    dn,
    upv,
    sel,
    upbuf,
    kbuf,
    cbuf,
    fwd1,
    fin1,
    c2,
    fin2,
    agbuf,
    ob,
    finx,
    xin,
    ubuf,
    half_slot,
    chunk_slot,
    qs,
    kns,
    vns,
    att,
    lrown,
    lrx,
    lrp,
    ssem,
    rsem,
    lsem,
    psend,
    precv,
    turn,
):
    s = lax.axis_index("section")
    t = lax.axis_index("tensor")
    p = lax.axis_index("pool")
    z = p // RING
    y = p % RING
    o = 1 - s
    outs = (first_ref, second_ref)

    def ring(i, d):
        return lax.rem(i + d + 2 * RING, RING)

    def at_z(j):
        return {"pool": j * RING + y}

    def at_y(j):
        return {"pool": z * RING + j}

    def at_x(j):
        return {"tensor": j}

    started = []
    used = [0]

    def remote(src, dst, dev):
        n = used[0]
        used[0] += 1
        assert n < N_SEM
        return pltpu.make_async_remote_copy(
            src_ref=src,
            dst_ref=dst,
            send_sem=ssem.at[n],
            recv_sem=rsem.at[n],
            device_id=dev,
            device_id_type=MESH,
        )

    def tracked(src, dst, dev):
        c = remote(src, dst, dev)
        started.append(c)
        return c

    def send(src, dst, dev):
        c = tracked(src, dst, dev)
        c.start()
        return c

    kvflat = wkv_hbm.reshape(2 * FEAT, KVCOLS)
    cflat = cache_hbm.reshape(2, OWN_ROWS, 2 * CTX, KVCOLS)
    load_x0 = [
        pltpu.make_async_copy(hidden_hbm.at[:, :, m], xin.at[0, m], lsem.at[(0, 9)[m]])
        for m in range(2)
    ]
    load_kv = pltpu.make_async_copy(kvflat, kvraw, lsem.at[1])
    load_wq = pltpu.make_async_copy(wq_hbm.at[0], wall.at[:, 0:QCOLS], lsem.at[2])
    load_up = pltpu.make_async_copy(up_hbm, upv, lsem.at[3])
    load_dn = pltpu.make_async_copy(down_hbm.at[:, s], dn.at[0], lsem.at[4])
    load_c = [
        pltpu.make_async_copy(cflat.at[k], kbuf.at[k], lsem.at[5 + k]) for k in range(2)
    ]
    load_wo = pltpu.make_async_copy(wo_hbm.at[0], wo.at[:, 0:FEAT], lsem.at[7])
    for c in load_x0:
        c.start()
    load_kv.start()
    load_wq.start()
    load_fresh = [
        pltpu.make_async_copy(fresh_hbm.at[:, :, m], xin.at[1, m], lsem.at[(8, 10)[m]])
        for m in range(2)
    ]

    barrier = pltpu.get_barrier_semaphore()

    def greet(d, _):
        pl.semaphore_signal(
            barrier, inc=1, device_id={"pool": lax.rem(p + d, 16)}, device_id_type=MESH
        )
        return _

    lax.fori_loop(1, 16, greet, 0)
    for d in range(1, RING):
        pl.semaphore_signal(
            barrier, inc=1, device_id={"tensor": ring(t, d)}, device_id_type=MESH
        )
    for d in range(RING):
        pl.semaphore_signal(
            barrier,
            inc=1,
            device_id={"section": o, "tensor": ring(t, d)},
            device_id_type=MESH,
        )

    load_kv.wait()
    pick_r = lax.broadcasted_iota(jnp.int32, (128, 256), 0)
    pick_c = lax.broadcasted_iota(jnp.int32, (128, 256), 1)
    for b in range(4):
        block = kvraw[b * 256 : (b + 1) * 256, :]
        for n in range(2):
            pick = jnp.where(pick_c == 2 * pick_r + n, 1.0, 0.0).astype(BF16)
            wall[
                b * 128 : (b + 1) * 128,
                QCOLS + n * KVCOLS : QCOLS + (n + 1) * KVCOLS,
            ] = dot(pick, block).astype(BF16)

    def project(k, m, begin=False, ready=None):
        xf = xin[k, m].reshape(256, FEAT).astype(F32)
        ubuf[...] = (xf * gain_ref[...]).astype(BF16)
        ss = jnp.sum(xf * xf, axis=1, keepdims=True)
        cbuf[k, m, :, :, :, QCOLS + 2 * KVCOLS : CW] = (
            jnp.broadcast_to(ss, (256, 128)).astype(BF16).reshape(4, 4, HALF_ROWS, 128)
        )

        def tile(n, _):
            cols = pl.ds(pl.multiple_of(n * 512, 512), 512)
            part = dot(ubuf[...], wall[:, cols])
            cbuf[k, m, :, :, :, cols] = part.astype(BF16).reshape(4, 4, HALF_ROWS, 512)
            return _

        lax.fori_loop(0, 3, tile, 0)
        if ready is not None:
            ready()
        if begin:
            rings[k][m][0][0].begin()
        lax.fori_loop(3, 5, tile, 0)
        if begin:
            rings[k][m][0][1].begin()

    class RingSum:
        def __init__(self, i, dev, src, fwd, fin):
            right, left = ring(i, 1), ring(i, -1)
            self.add0, self.fwd0 = src(right, 0), fwd(0)
            self.add1, self.fwd1 = src(left, 1), fwd(1)
            self.f0 = tracked(src(ring(i, 2), 0), fwd(0), dev(right))
            self.f1 = tracked(src(ring(i, 2), 1), fwd(1), dev(left))
            self.a0 = tracked(src(right, 1), fin(0, 1), dev(right))
            self.a1 = tracked(src(left, 0), fin(1, 0), dev(left))
            self.b0 = tracked(self.add0, fin(0, 0), dev(right))
            self.b1 = tracked(self.add1, fin(1, 1), dev(left))
            self.copies = [self.f0, self.f1, self.a0, self.a1, self.b0, self.b1]

        def begin(self):
            for c in (self.f0, self.f1, self.a0, self.a1):
                c.start()

        def middle(self):
            self.f0.wait_recv()
            v, w = self.add0, self.fwd0
            v[...] = (v[...].astype(F32) + w[...].astype(F32)).astype(BF16)
            self.b0.start()
            self.f1.wait_recv()
            v, w = self.add1, self.fwd1
            v[...] = (v[...].astype(F32) + w[...].astype(F32)).astype(BF16)
            self.b1.start()

        def end(self):
            for c in (self.a0, self.a1, self.b0, self.b1):
                c.wait_recv()

    class RingGather:
        def __init__(self, i, dev, block):
            right, left = ring(i, 1), ring(i, -1)
            self.r0 = tracked(block(i, 0), block(i, 0), dev(right))
            self.l1 = tracked(block(i, 1), block(i, 1), dev(left))
            self.r1 = tracked(block(i, 1), block(i, 1), dev(right))
            self.l0 = tracked(block(i, 0), block(i, 0), dev(left))
            self.f0 = tracked(block(left, 0), block(left, 0), dev(right))
            self.f1 = tracked(block(right, 1), block(right, 1), dev(left))
            self.copies = [self.r0, self.l1, self.r1, self.l0, self.f0, self.f1]

        def begin(self):
            for c in (self.r0, self.l1, self.r1, self.l0):
                c.start()

        def middle(self):
            self.r0.wait_recv()
            self.f0.start()
            self.l1.wait_recv()
            self.f1.start()

        def end(self):
            for c in (self.r1, self.l0, self.f0, self.f1):
                c.wait_recv()

    class DirectSum:
        def __init__(self, i, dev, src, fin):
            self.copies = [
                tracked(src(ring(i, d)), fin(d - 1), dev(ring(i, d))) for d in (2, 1, 3)
            ]

        def begin(self):
            for c in self.copies:
                c.start()

        def end(self):
            for c in self.copies:
                c.wait_recv()

    class DirectGather:
        def __init__(self, i, dev, block):
            self.copies = [
                tracked(block(i), block(i), dev(ring(i, d))) for d in (2, 1, 3)
            ]

        def begin(self):
            for c in self.copies:
                c.start()

        def end(self):
            for c in self.copies:
                c.wait_recv()

    def pool_rings(k, m):
        def cols(n):
            return slice(STARTS[n], STARTS[n] + WIDTHS[n])

        def own(n):
            return slice(0, WIDTHS[n])

        first = [
            RingSum(
                z,
                at_z,
                lambda j, hf: cbuf.at[k, m, j, 2 * hf : 2 * hf + 2, :, cols(0)],
                lambda d: fwd1.at[k, m, 0, d, :, :, own(0)],
                lambda d, hf: fin1.at[k, m, 0, d, 2 * hf : 2 * hf + 2, :, own(0)],
            ),
            RingSum(
                y,
                at_y,
                lambda j, hf: cbuf.at[k, m, 2 * hf : 2 * hf + 2, j, :, cols(1)],
                lambda d: fwd1.at[k, m, 1, d, :, :, own(1)],
                lambda d, hf: fin1.at[k, m, 1, d, 2 * hf : 2 * hf + 2, :, own(1)],
            ),
        ]
        second = [
            DirectSum(
                (y, z)[n],
                (at_y, at_z)[n],
                lambda j, n=n: c2.at[k, m, n, j, :, own(n)],
                lambda c, n=n: fin2.at[k, m, n, c, :, own(n)],
            )
            for n in range(2)
        ]
        return first, second

    def sum_begin(k, m):
        for r in rings[k][m][0]:
            r.begin()

    def sum_middle(k, m):
        for r in rings[k][m][0]:
            r.middle()

    def sum_second(k, m):
        first, second = rings[k][m]
        for n in range(2):
            first[n].end()
            cols = slice(STARTS[n], STARTS[n] + WIDTHS[n])
            own = slice(0, WIDTHS[n])
            for b in range(RING):
                mine = cbuf[k, m, z, b, :, cols] if n == 0 else cbuf[k, m, b, y, :, cols]
                c2[k, m, n, b, :, own] = (
                    mine.astype(F32)
                    + fin1[k, m, n, 0, b, :, own].astype(F32)
                    + fin1[k, m, n, 1, b, :, own].astype(F32)
                ).astype(BF16)
            second[n].begin()

    def sum_end(k, m):
        totals = []
        for n in range(2):
            rings[k][m][1][n].end()
            own = slice(0, WIDTHS[n])
            total = c2[k, m, n, y if n == 0 else z, :, own].astype(F32)
            for c in range(3):
                total = total + fin2[k, m, n, c, :, own].astype(F32)
            totals.append(total)
        total = jnp.concatenate(totals, axis=1)
        rstd = lax.rsqrt(total[:, QCOLS + 2 * KVCOLS :] * (1.0 / MODEL) + NORM_EPS)

        def part(n):
            return (total[:, n * HEAD : (n + 1) * HEAD] * rstd).astype(BF16).astype(F32)

        keys = [part(HEADS + g) for g in range(2)]
        values = [part(HEADS + 2 + g) for g in range(2)]
        for n in range(HEADS):
            at = pl.ds(m * HALF_ROWS * HEADS + n, HALF_ROWS, stride=HEADS)
            qs[at, :] = part(n)
            kns[at, :] = keys[n // 8]
            vns[at, :] = values[n // 8]

    inv_scale = 1.0 / math.sqrt(HEAD)
    group = 128 // HEADS
    lane = lax.broadcasted_iota(jnp.int32, (1, 128), 1)
    lane_row = lane // HEADS
    low_heads = lane - lane_row * HEADS < 8
    position = lax.broadcasted_iota(jnp.int32, (2 * CTX, 128), 0)
    even = (position & 1) == 0

    def attention(k, i):
        at = slice(i * 128, (i + 1) * 128)
        q = qs[at, :]
        own = jnp.exp(jnp.sum(q * kns[at, :], axis=1, keepdims=True) * inv_scale)
        qt = q.T
        wide = jnp.concatenate(
            [jnp.where(low_heads, qt, 0.0), jnp.where(low_heads, 0.0, qt)], axis=0
        )
        length = jnp.zeros((1, 128), jnp.int32)
        scores = jnp.zeros((2 * CTX, 128), F32)
        for r in range(group):
            mine = lane_row == r
            scores = scores + dot(
                kbuf[k, i * group + r], jnp.where(mine, wide, 0.0).astype(BF16)
            )
            length = jnp.where(
                mine, len_ref[s + 1 - k, p * OWN_ROWS + i * group + r], length
            )
        live = even & (position < 2 * length)
        weights = jnp.where(live, jnp.exp(jnp.where(live, scores, 0.0) * inv_scale), 0.0)
        weights = pltpu.roll(weights, 1, 0).T
        den = jnp.sum(weights, axis=1, keepdims=True) + own
        weights = weights.astype(BF16)
        nums = []
        for r in range(group):
            pv = dot(weights[r * HEADS : (r + 1) * HEADS], kbuf[k, i * group + r])
            nums += [pv[:8, :HEAD], pv[8:, HEAD:]]
        num = jnp.concatenate(nums, axis=0) + own.astype(BF16).astype(F32) * vns[at, :]
        att[at, :] = num / den

    def attended(k, m):
        for n in range(HEADS):
            at = pl.ds(m * HALF_ROWS * HEADS + n, HALF_ROWS, stride=HEADS)
            agbuf[k, m, z, y, :, n * HEAD : (n + 1) * HEAD] = att[at, :].astype(BF16)

    def gather_rings(k, m):
        low, high = slice(0, QCOLS // 2), slice(QCOLS // 2, QCOLS)
        first = [
            DirectGather(y, at_y, lambda j: agbuf.at[k, m, z, j, :, low]),
            DirectGather(z, at_z, lambda j: agbuf.at[k, m, j, y, :, high]),
        ]
        second = [
            RingGather(
                z, at_z, lambda j, hf: agbuf.at[k, m, j, 2 * hf : 2 * hf + 2, :, low]
            ),
            RingGather(
                y, at_y, lambda j, hf: agbuf.at[k, m, 2 * hf : 2 * hf + 2, j, :, high]
            ),
        ]
        return first, second

    def gather_begin(k, m):
        for r in gathers[k][m][0]:
            r.begin()

    def gather_second(k, m):
        first, second = gathers[k][m]
        for n in range(2):
            first[n].end()
            second[n].begin()

    def gather_middle(k, m):
        for r in gathers[k][m][1]:
            r.middle()

    def gather_end(k, m):
        for r in gathers[k][m][1]:
            r.end()

    def down_product(k, m):
        rows = agbuf[k, m].reshape(256, QCOLS)
        down = dot(rows, wo[:, FEAT:]).T
        ids = half_slot[k, m, 0:1, :]
        acc = jnp.zeros((RANK, 256), F32)
        for n in range(16):
            slot = ((s if n < 8 else o) * 16 + p) * 8 + n % 8
            acc = acc + jnp.where(ids == slot, down[n * RANK : (n + 1) * RANK, :], 0.0)
        pad = jnp.zeros((RANK, 64), F32)
        for j in range(RING):
            lrown[k, m, j] = jnp.concatenate([acc[:, j * 64 : (j + 1) * 64], pad], axis=1)
        for c in lows[k][m]:
            c.start()

    def out_product(k, m):
        rows = agbuf[k, m].reshape(256, QCOLS)
        ob[k, m] = dot(rows, wo[:, :FEAT]).astype(BF16).reshape(4, 4, HALF_ROWS, FEAT)
        for d in (2, 1, 3):
            tops[k][m][d - 1].start()

    def low_copy(k, m, d):
        return pltpu.make_async_remote_copy(
            src_ref=lrp.at[k, m, p],
            dst_ref=lrp.at[k, m, p],
            send_sem=psend.at[k, m, d],
            recv_sem=precv.at[k, m, d],
            device_id={"pool": lax.rem(p + d, 16)},
            device_id_type=MESH,
        )

    def output_low(k, m):
        total = lrown[k, m, t]
        for d in range(1, RING):
            lows[k][m][d - 1].wait_recv()
            total = total + lrx[k, m, ring(t, -d)]
        lrp[k, m, p] = total.astype(BF16)

        def give(d, _):
            low_copy(k, m, d).start()
            return _

        lax.fori_loop(1, 16, give, 0)

    def output_delta(k, m):
        def receive(d, _):
            low_copy(k, m, d).wait()
            return _

        lax.fori_loop(1, 16, receive, 0)
        low_rank = lrp[k, m, 0].astype(F32)
        for n in range(1, 16):
            low_rank = low_rank + lrp[k, m, n].astype(F32)
        if m == 0:
            for c in panels[k]:
                c.wait_recv()
        block = lax.shift_right_logical(chunk_slot[k, m, t, 0:1, :], 3)
        wide = jnp.concatenate(
            [jnp.where(block == b, low_rank, 0.0) for b in range(32)], axis=0
        )
        delta = dot(wide.T[:64].astype(BF16), upbuf[k].reshape(512, FEAT))
        total = xin[k, m, t].astype(F32) + ob[k, m, t].astype(F32)
        for c in tops[k][m]:
            c.wait_recv()
        for d in range(3):
            total = total + finx[k, m, d].astype(F32)
        outs[k][0, :, m] = (
            total + ADAPTER_SCALE * delta.reshape(RING, HALF_ROWS, FEAT)
        ).astype(BF16)

    def slots_and_offsets():
        ids = [aor_ref[pl.ds(s + 1 - k, 1), :] for k in range(2)]
        first_block = (s * RING + t) * 4

        def step(a, carry):
            rows, offs = carry
            slots = [table_ref[apb_ref[c, a]] for c in range(3)]
            new_offs = []
            for c in range(3):
                block = lax.shift_right_logical(slots[c], 3) - first_block
                new_offs += [
                    jnp.where(block == j, slots[c] & 7, offs[4 * c + j]) for j in range(4)
                ]
            new_rows = []
            for k in range(2):
                slot = jnp.where(s == 0, slots[1 - k], slots[2 - k])
                new_rows.append(jnp.where(ids[k] == a, slot, rows[k]))
            return tuple(new_rows), tuple(new_offs)

        rows, offs = lax.fori_loop(
            0,
            32,
            step,
            ((jnp.zeros((1, ROWS), jnp.int32),) * 2, (jnp.int32(0),) * 12),
        )
        for k in range(2):

            def piece(j, b, m):
                at = (j * RING + b) * OWN_ROWS + m * HALF_ROWS
                return rows[k][:, at : at + HALF_ROWS]

            for m in range(2):
                half_slot[k, m, 0:1, :] = jnp.concatenate(
                    [piece(j, b, m) for j in range(RING) for b in range(RING)], axis=1
                )
                for j in range(RING):
                    part = jnp.concatenate([piece(j, b, m) for b in range(RING)], axis=1)
                    chunk_slot[k, m, j, 0:1, :] = jnp.concatenate([part, part], axis=1)
        return offs

    panels = [[], []]
    holder = s * RING + t
    for w in range(2):
        for k in range(2):
            for d in range(1 if w == 0 else 0, RING):
                panels[k].append(
                    tracked(
                        sel.at[w, k],
                        upbuf.at[k, holder],
                        {"section": s if w == 0 else o, "tensor": ring(t, d)},
                    )
                )

    def give_panels(offs):
        load_up.wait()
        for w in range(2):
            layer = s if w == 0 else o
            for k in range(2):
                for j in range(4):
                    off = jnp.where(layer == 0, offs[4 * (1 - k) + j], offs[4 * (2 - k) + j])
                    sel[w, k, j * RANK : (j + 1) * RANK, :] = upv[8 * j + off, layer]
                if w == 0:
                    upbuf[k, holder] = sel[w, k]
        for k in range(2):
            for c in panels[k]:
                c.start()

    def spread_down():
        for n in range(2):
            for m in range(QCOLS // 128):
                panel = dn[n, :, :, m * 128 : (m + 1) * 128].reshape(8 * RANK, 128)
                wo[m * 128 : (m + 1) * 128, FEAT + n * 128 : FEAT + (n + 1) * 128] = (
                    panel.astype(F32).T.astype(BF16)
                )

    rings = [[pool_rings(k, m) for m in range(2)] for k in range(2)]
    gathers = [[gather_rings(k, m) for m in range(2)] for k in range(2)]
    lows = [
        [
            [
                tracked(lrown.at[k, m, ring(t, d)], lrx.at[k, m, t], at_x(ring(t, d)))
                for d in range(1, RING)
            ]
            for m in range(2)
        ]
        for k in range(2)
    ]
    tops = [
        [
            [
                tracked(ob.at[k, m, ring(t, d)], finx.at[k, m, d - 1], at_x(ring(t, d)))
                for d in range(1, RING)
            ]
            for m in range(2)
        ]
        for k in range(2)
    ]

    def drain(copies):
        for c in copies:
            c.wait_send()
            started[:] = [other for other in started if other is not c]

    def ring_copies(which):
        return [
            c
            for m in range(2)
            for stage in which[m]
            for r in stage
            for c in r.copies
        ]

    for c in load_x0:
        c.wait()
    load_wq.wait()
    load_up.start()
    load_c[0].start()

    @pl.when(s == 0)
    def _():
        for c in load_fresh:
            c.start()

    load_wo.start()
    load_dn.start()
    load_c[1].start()
    other_down = tracked(down_hbm.at[:, o], dn.at[1], {"section": o})

    def everyone_is_here():
        pl.semaphore_wait(barrier, 22)

    @pl.when(s == 0)
    def _():
        project(0, 0, begin=True, ready=everyone_is_here)
        other_down.start()
        project(0, 1)
        sum_middle(0, 0)
        sum_begin(0, 1)
        offs = slots_and_offsets()
        sum_middle(0, 1)
        sum_second(0, 0)
        give_panels(offs)
        for c in load_fresh:
            c.wait()
        project(1, 0)

    @pl.when(s == 1)
    def _():
        project(0, 0)
        everyone_is_here()
        other_down.start()
        project(0, 1)
        give_panels(slots_and_offsets())
        pl.semaphore_wait(turn, 1)
        sum_begin(0, 0)
        sum_middle(0, 0)
        sum_begin(0, 1)
        sum_middle(0, 1)
        sum_second(0, 0)

    sum_end(0, 0)
    sum_second(0, 1)

    @pl.when(s == 0)
    def _():
        pl.semaphore_signal(turn, inc=1, device_id={"section": o}, device_id_type=MESH)

    load_c[0].wait()
    attention(0, 0)
    attention(0, 1)
    attended(0, 0)
    gather_begin(0, 0)
    sum_end(0, 1)
    attention(0, 2)
    gather_second(0, 0)
    attention(0, 3)
    attended(0, 1)
    gather_begin(0, 1)
    gather_middle(0, 0)
    gather_second(0, 1)
    load_dn.wait()
    other_down.wait_recv()
    load_wo.wait()
    spread_down()
    gather_end(0, 0)
    gather_middle(0, 1)

    @pl.when(s == 0)
    def _():
        sum_begin(1, 0)
        project(1, 1)

    down_product(0, 0)
    out_product(0, 0)

    relay = [
        [
            remote(
                first_ref.at[0, :, m], xin.at[1, m, t], {"section": 1, "tensor": ring(t, d)}
            )
            for d in range(RING)
        ]
        for m in range(2)
    ]

    def relay_start(m):
        for d in (2, 1, 3, 0):
            relay[m][d].start()

    def relay_wait(m):
        for c in relay[m]:
            c.wait_recv()

    @pl.when(s == 0)
    def _():
        output_low(0, 0)
        gather_end(0, 1)
        down_product(0, 1)
        output_delta(0, 0)
        relay_start(0)
        sum_middle(1, 0)
        sum_begin(1, 1)
        out_product(0, 1)
        output_low(0, 1)
        sum_middle(1, 1)
        output_delta(0, 1)
        relay_start(1)
        sum_second(1, 0)
        for m in range(2):
            for c in relay[m]:
                c.wait_send()

    @pl.when(s == 1)
    def _():
        output_low(0, 0)
        gather_end(0, 1)
        relay_wait(0)
        project(1, 0, begin=True)
        down_product(0, 1)
        sum_middle(1, 0)
        relay_wait(1)
        project(1, 1)
        sum_begin(1, 1)
        sum_second(1, 0)
        out_product(0, 1)
        sum_middle(1, 1)
        output_low(0, 1)
        output_delta(0, 0)

    sum_end(1, 0)
    sum_second(1, 1)
    load_c[1].wait()
    attention(1, 0)
    attention(1, 1)
    attended(1, 0)
    gather_begin(1, 0)
    sum_end(1, 1)
    attention(1, 2)
    gather_second(1, 0)
    attention(1, 3)
    attended(1, 1)
    gather_begin(1, 1)
    gather_middle(1, 0)
    drain(ring_copies(rings[0]))
    gather_second(1, 1)

    @pl.when(s == 1)
    def _():
        output_delta(0, 1)

    gather_end(1, 0)
    gather_middle(1, 1)
    drain(ring_copies(gathers[0]))
    down_product(1, 0)
    out_product(1, 0)
    output_low(1, 0)
    drain([other_down] + lows[0][0] + lows[0][1] + panels[0] + panels[1])
    drain(tops[0][0] + tops[0][1])
    gather_end(1, 1)
    down_product(1, 1)
    out_product(1, 1)
    output_delta(1, 0)
    output_low(1, 1)
    drain(ring_copies(rings[1]))
    drain(ring_copies(gathers[1]))
    output_delta(1, 1)
    drain(list(started))


def hand_over(first_in, second_in, first_out, second_out):
    first_out[...] = first_in[...]
    second_out[...] = second_in[...]


def on_device(hidden_input, fresh, *args):
    rows = (RING, RING, 2, HALF_ROWS, FEAT)
    any_space = pl.BlockSpec(memory_space=pl.ANY)
    vmem = pl.BlockSpec(memory_space=pltpu.VMEM)
    smem = pl.BlockSpec(memory_space=pltpu.SMEM)
    out = jax.ShapeDtypeStruct((1, RING, 2, HALF_ROWS, FEAT), BF16)
    v = pltpu.VMEM
    dma = pltpu.SemaphoreType.DMA
    first, second = pl.pallas_call(
        kernel,
        out_shape=(out, out),
        in_specs=[
            any_space,
            any_space,
            vmem,
            any_space,
            any_space,
            any_space,
            any_space,
            smem,
            vmem,
            smem,
            smem,
            any_space,
            any_space,
        ],
        out_specs=(vmem, vmem),
        scratch_shapes=[
            v((FEAT, QCOLS + 2 * KVCOLS), BF16),
            v((2 * FEAT, KVCOLS), BF16),
            v((QCOLS, FEAT + 16 * RANK), BF16),
            v((2, 8, RANK, QCOLS), BF16),
            v((32, 2, RANK, FEAT), BF16),
            v((2, 2, 4 * RANK, FEAT), BF16),
            v((2, 8, 4 * RANK, FEAT), BF16),
            v((2, OWN_ROWS, 2 * CTX, KVCOLS), BF16),
            v((2, 2, RING, RING, HALF_ROWS, CW), BF16),
            v((2, 2, 2, 2, 2, HALF_ROWS, WIDTHS[0]), BF16),
            v((2, 2, 2, 2, RING, HALF_ROWS, WIDTHS[0]), BF16),
            v((2, 2, 2, RING, HALF_ROWS, WIDTHS[0]), BF16),
            v((2, 2, 2, 3, HALF_ROWS, WIDTHS[0]), BF16),
            v((2, 2, RING, RING, HALF_ROWS, QCOLS), BF16),
            v((2, 2, RING, RING, HALF_ROWS, FEAT), BF16),
            v((2, 2, 3, RING, HALF_ROWS, FEAT), BF16),
            v((2, 2, RING, RING, HALF_ROWS, FEAT), BF16),
            v((ROWS // 2, FEAT), BF16),
            v((2, 2, 8, 256), jnp.int32),
            v((2, 2, RING, 8, 128), jnp.int32),
            v((OWN_ROWS * HEADS, HEAD), F32),
            v((OWN_ROWS * HEADS, HEAD), F32),
            v((OWN_ROWS * HEADS, HEAD), F32),
            v((OWN_ROWS * HEADS, HEAD), F32),
            v((2, 2, RING, RANK, 128), F32),
            v((2, 2, RING, RANK, 128), F32),
            v((2, 2, 16, RANK, 128), BF16),
            dma((N_SEM,)),
            dma((N_SEM,)),
            dma((11,)),
            dma((2, 2, 16)),
            dma((2, 2, 16)),
            pltpu.SemaphoreType.REGULAR,
        ],
        compiler_params=pltpu.CompilerParams(
            collective_id=0, has_side_effects=True, vmem_limit_bytes=58 * 2**20
        ),
        cost_estimate=pl.CostEstimate(
            flops=8_000_000_000, bytes_accessed=16_000_000, transcendentals=500_000
        ),
    )(hidden_input.reshape(rows), fresh.reshape(rows), *args)
    first, second = pl.pallas_call(
        hand_over,
        out_shape=(out, out),
        in_specs=[vmem, vmem],
        out_specs=(vmem, vmem),
    )(first, second)
    return first.reshape(1, 128, FEAT), second.reshape(1, 128, FEAT)


def solution(mesh):
    return jax.shard_map(
        on_device,
        mesh=mesh,
        in_specs=(
            P("section", None, "pool"),
            P(None, "pool"),
            P("section", "pool"),
            P("section", "pool", "tensor"),
            P("section", "pool", None, "tensor"),
            P("section", "tensor", "pool"),
            P("section", None, "pool", None, None, "tensor"),
            P(),
            P(),
            P(),
            P(),
            P(("section", "pool"), None, None, "tensor"),
            P(("section", "tensor"), None, None, "pool"),
        ),
        out_specs=(P("section", "tensor", "pool"), P("section", "tensor", "pool")),
        check_vma=False,
    )
```

```python
import functools
import math

import jax
import jax.numpy as jnp
from jax import lax
from jax.experimental import pallas as pl
from jax.experimental.pallas import tpu as pltpu
from jax.sharding import PartitionSpec as P

NORM_EPS = 1e-05
ADAPTER_SCALE = 2.0
MESH = pl.DeviceIdType.MESH
F32 = jnp.float32
BF16 = jnp.bfloat16

RING = 4
ROWS = 512
FEAT = 512
MODEL = 8192
QCOLS = 2048
KVCOLS = 256
HEADS = 16
HEAD = 128
CTX = 128
CW = QCOLS + 2 * KVCOLS + 128
WIDTHS = (1408, CW - 1408)
STARTS = (0, 1408)
OWN_ROWS = 32
HALF_ROWS = 16
RANK = 16
N_SEM = 224


def dot(a, b):
    return jnp.dot(a, b, preferred_element_type=F32)


def kernel(
    hidden_hbm,
    fresh_hbm,
    gain_ref,
    wq_hbm,
    wkv_hbm,
    wo_hbm,
    cache_hbm,
    len_ref,
    aor_ref,
    apb_ref,
    table_ref,
    down_hbm,
    up_hbm,
    first_ref,
    second_ref,
    wall,
    kvraw,
    wo,
    dn,
    upv,
    sel,
    upbuf,
    kbuf,
    cbuf,
    fwd1,
    fin1,
    c2,
    fin2,
    agbuf,
    ob,
    finx,
    xin,
    ubuf,
    half_slot,
    chunk_slot,
    qs,
    kns,
    vns,
    att,
    lrown,
    lrx,
    lrp,
    ssem,
    rsem,
    lsem,
    psend,
    precv,
    turn,
):
    s = lax.axis_index("section")
    t = lax.axis_index("tensor")
    p = lax.axis_index("pool")
    z = p // RING
    y = p % RING
    o = 1 - s
    outs = (first_ref, second_ref)

    def ring(i, d):
        return lax.rem(i + d + 2 * RING, RING)

    def at_z(j):
        return {"pool": j * RING + y}

    def at_y(j):
        return {"pool": z * RING + j}

    def at_x(j):
        return {"tensor": j}

    started = []
    used = [0]

    def remote(src, dst, dev):
        n = used[0]
        used[0] += 1
        assert n < N_SEM
        return pltpu.make_async_remote_copy(
            src_ref=src,
            dst_ref=dst,
            send_sem=ssem.at[n],
            recv_sem=rsem.at[n],
            device_id=dev,
            device_id_type=MESH,
        )

    def tracked(src, dst, dev):
        c = remote(src, dst, dev)
        started.append(c)
        return c

    def send(src, dst, dev):
        c = tracked(src, dst, dev)
        c.start()
        return c

    kvflat = wkv_hbm.reshape(2 * FEAT, KVCOLS)
    cflat = cache_hbm.reshape(2, OWN_ROWS, 2 * CTX, KVCOLS)
    load_x0 = [
        pltpu.make_async_copy(hidden_hbm.at[:, :, m], xin.at[0, m], lsem.at[(0, 9)[m]])
        for m in range(2)
    ]
    load_kv = pltpu.make_async_copy(kvflat, kvraw, lsem.at[1])
    load_wq = pltpu.make_async_copy(wq_hbm.at[0], wall.at[:, 0:QCOLS], lsem.at[2])
    load_up = pltpu.make_async_copy(up_hbm, upv, lsem.at[3])
    load_dn = pltpu.make_async_copy(down_hbm.at[:, s], dn.at[0], lsem.at[4])
    load_c = [
        pltpu.make_async_copy(cflat.at[k], kbuf.at[k], lsem.at[5 + k]) for k in range(2)
    ]
    load_wo = pltpu.make_async_copy(wo_hbm.at[0], wo.at[:, 0:FEAT], lsem.at[7])
    for c in load_x0:
        c.start()
    load_kv.start()
    load_wq.start()
    load_fresh = [
        pltpu.make_async_copy(fresh_hbm.at[:, :, m], xin.at[1, m], lsem.at[(8, 10)[m]])
        for m in range(2)
    ]

    barrier = pltpu.get_barrier_semaphore()

    def greet(d, _):
        pl.semaphore_signal(
            barrier, inc=1, device_id={"pool": lax.rem(p + d, 16)}, device_id_type=MESH
        )
        return _

    lax.fori_loop(1, 16, greet, 0)
    for d in range(1, RING):
        pl.semaphore_signal(
            barrier, inc=1, device_id={"tensor": ring(t, d)}, device_id_type=MESH
        )
    for d in range(RING):
        pl.semaphore_signal(
            barrier,
            inc=1,
            device_id={"section": o, "tensor": ring(t, d)},
            device_id_type=MESH,
        )

    load_kv.wait()
    pick_r = lax.broadcasted_iota(jnp.int32, (128, 256), 0)
    pick_c = lax.broadcasted_iota(jnp.int32, (128, 256), 1)
    for b in range(4):
        block = kvraw[b * 256 : (b + 1) * 256, :]
        for n in range(2):
            pick = jnp.where(pick_c == 2 * pick_r + n, 1.0, 0.0).astype(BF16)
            wall[
                b * 128 : (b + 1) * 128,
                QCOLS + n * KVCOLS : QCOLS + (n + 1) * KVCOLS,
            ] = dot(pick, block).astype(BF16)

    def project(k, m, begin=False, ready=None):
        xf = xin[k, m].reshape(256, FEAT).astype(F32)
        ubuf[...] = (xf * gain_ref[...]).astype(BF16)
        ss = jnp.sum(xf * xf, axis=1, keepdims=True)
        cbuf[k, m, :, :, :, QCOLS + 2 * KVCOLS : CW] = (
            jnp.broadcast_to(ss, (256, 128)).astype(BF16).reshape(4, 4, HALF_ROWS, 128)
        )

        def tile(n, _):
            cols = pl.ds(pl.multiple_of(n * 512, 512), 512)
            part = dot(ubuf[...], wall[:, cols])
            cbuf[k, m, :, :, :, cols] = part.astype(BF16).reshape(4, 4, HALF_ROWS, 512)
            return _

        lax.fori_loop(0, 3, tile, 0)
        if ready is not None:
            ready()
        if begin:
            rings[k][m][0][0].begin()
        lax.fori_loop(3, 5, tile, 0)
        if begin:
            rings[k][m][0][1].begin()

    class RingSum:
        def __init__(self, i, dev, src, fwd, fin):
            right, left = ring(i, 1), ring(i, -1)
            self.add0, self.fwd0 = src(right, 0), fwd(0)
            self.add1, self.fwd1 = src(left, 1), fwd(1)
            self.f0 = tracked(src(ring(i, 2), 0), fwd(0), dev(right))
            self.f1 = tracked(src(ring(i, 2), 1), fwd(1), dev(left))
            self.a0 = tracked(src(right, 1), fin(0, 1), dev(right))
            self.a1 = tracked(src(left, 0), fin(1, 0), dev(left))
            self.b0 = tracked(self.add0, fin(0, 0), dev(right))
            self.b1 = tracked(self.add1, fin(1, 1), dev(left))
            self.copies = [self.f0, self.f1, self.a0, self.a1, self.b0, self.b1]

        def begin(self):
            for c in (self.f0, self.f1, self.a0, self.a1):
                c.start()

        def middle(self):
            self.f0.wait_recv()
            v, w = self.add0, self.fwd0
            v[...] = (v[...].astype(F32) + w[...].astype(F32)).astype(BF16)
            self.b0.start()
            self.f1.wait_recv()
            v, w = self.add1, self.fwd1
            v[...] = (v[...].astype(F32) + w[...].astype(F32)).astype(BF16)
            self.b1.start()

        def end(self):
            for c in (self.a0, self.a1, self.b0, self.b1):
                c.wait_recv()

    class RingGather:
        def __init__(self, i, dev, block):
            right, left = ring(i, 1), ring(i, -1)
            self.r0 = tracked(block(i, 0), block(i, 0), dev(right))
            self.l1 = tracked(block(i, 1), block(i, 1), dev(left))
            self.r1 = tracked(block(i, 1), block(i, 1), dev(right))
            self.l0 = tracked(block(i, 0), block(i, 0), dev(left))
            self.f0 = tracked(block(left, 0), block(left, 0), dev(right))
            self.f1 = tracked(block(right, 1), block(right, 1), dev(left))
            self.copies = [self.r0, self.l1, self.r1, self.l0, self.f0, self.f1]

        def begin(self):
            for c in (self.r0, self.l1, self.r1, self.l0):
                c.start()

        def middle(self):
            self.r0.wait_recv()
            self.f0.start()
            self.l1.wait_recv()
            self.f1.start()

        def end(self):
            for c in (self.r1, self.l0, self.f0, self.f1):
                c.wait_recv()

    class DirectSum:
        def __init__(self, i, dev, src, fin):
            self.copies = [
                tracked(src(ring(i, d)), fin(d - 1), dev(ring(i, d))) for d in (2, 1, 3)
            ]

        def begin(self):
            for c in self.copies:
                c.start()

        def end(self):
            for c in self.copies:
                c.wait_recv()

    class DirectGather:
        def __init__(self, i, dev, block):
            self.copies = [
                tracked(block(i), block(i), dev(ring(i, d))) for d in (2, 1, 3)
            ]

        def begin(self):
            for c in self.copies:
                c.start()

        def end(self):
            for c in self.copies:
                c.wait_recv()

    def pool_rings(k, m):
        def cols(n):
            return slice(STARTS[n], STARTS[n] + WIDTHS[n])

        def own(n):
            return slice(0, WIDTHS[n])

        first = [
            RingSum(
                z,
                at_z,
                lambda j, hf: cbuf.at[k, m, j, 2 * hf : 2 * hf + 2, :, cols(0)],
                lambda d: fwd1.at[k, m, 0, d, :, :, own(0)],
                lambda d, hf: fin1.at[k, m, 0, d, 2 * hf : 2 * hf + 2, :, own(0)],
            ),
            RingSum(
                y,
                at_y,
                lambda j, hf: cbuf.at[k, m, 2 * hf : 2 * hf + 2, j, :, cols(1)],
                lambda d: fwd1.at[k, m, 1, d, :, :, own(1)],
                lambda d, hf: fin1.at[k, m, 1, d, 2 * hf : 2 * hf + 2, :, own(1)],
            ),
        ]
        second = [
            DirectSum(
                (y, z)[n],
                (at_y, at_z)[n],
                lambda j, n=n: c2.at[k, m, n, j, :, own(n)],
                lambda c, n=n: fin2.at[k, m, n, c, :, own(n)],
            )
            for n in range(2)
        ]
        return first, second

    def sum_begin(k, m):
        for r in rings[k][m][0]:
            r.begin()

    def sum_middle(k, m):
        for r in rings[k][m][0]:
            r.middle()

    def sum_second(k, m):
        first, second = rings[k][m]
        for n in range(2):
            first[n].end()
            cols = slice(STARTS[n], STARTS[n] + WIDTHS[n])
            own = slice(0, WIDTHS[n])
            for b in range(RING):
                mine = cbuf[k, m, z, b, :, cols] if n == 0 else cbuf[k, m, b, y, :, cols]
                c2[k, m, n, b, :, own] = (
                    mine.astype(F32)
                    + fin1[k, m, n, 0, b, :, own].astype(F32)
                    + fin1[k, m, n, 1, b, :, own].astype(F32)
                ).astype(BF16)
            second[n].begin()

    def sum_end(k, m):
        totals = []
        for n in range(2):
            rings[k][m][1][n].end()
            own = slice(0, WIDTHS[n])
            total = c2[k, m, n, y if n == 0 else z, :, own].astype(F32)
            for c in range(3):
                total = total + fin2[k, m, n, c, :, own].astype(F32)
            totals.append(total)
        total = jnp.concatenate(totals, axis=1)
        rstd = lax.rsqrt(total[:, QCOLS + 2 * KVCOLS :] * (1.0 / MODEL) + NORM_EPS)

        def part(n):
            return (total[:, n * HEAD : (n + 1) * HEAD] * rstd).astype(BF16).astype(F32)

        keys = [part(HEADS + g) for g in range(2)]
        values = [part(HEADS + 2 + g) for g in range(2)]
        for n in range(HEADS):
            at = pl.ds(m * HALF_ROWS * HEADS + n, HALF_ROWS, stride=HEADS)
            qs[at, :] = part(n)
            kns[at, :] = keys[n // 8]
            vns[at, :] = values[n // 8]

    inv_scale = 1.0 / math.sqrt(HEAD)
    group = 128 // HEADS
    lane = lax.broadcasted_iota(jnp.int32, (1, 128), 1)
    lane_row = lane // HEADS
    low_heads = lane - lane_row * HEADS < 8
    position = lax.broadcasted_iota(jnp.int32, (2 * CTX, 128), 0)
    even = (position & 1) == 0

    def attention(k, i):
        at = slice(i * 128, (i + 1) * 128)
        q = qs[at, :]
        own = jnp.exp(jnp.sum(q * kns[at, :], axis=1, keepdims=True) * inv_scale)
        qt = q.T
        wide = jnp.concatenate(
            [jnp.where(low_heads, qt, 0.0), jnp.where(low_heads, 0.0, qt)], axis=0
        )
        length = jnp.zeros((1, 128), jnp.int32)
        scores = jnp.zeros((2 * CTX, 128), F32)
        for r in range(group):
            mine = lane_row == r
            scores = scores + dot(
                kbuf[k, i * group + r], jnp.where(mine, wide, 0.0).astype(BF16)
            )
            length = jnp.where(
                mine, len_ref[s + 1 - k, p * OWN_ROWS + i * group + r], length
            )
        live = even & (position < 2 * length)
        weights = jnp.where(live, jnp.exp(jnp.where(live, scores, 0.0) * inv_scale), 0.0)
        weights = pltpu.roll(weights, 1, 0).T
        den = jnp.sum(weights, axis=1, keepdims=True) + own
        weights = weights.astype(BF16)
        nums = []
        for r in range(group):
            pv = dot(weights[r * HEADS : (r + 1) * HEADS], kbuf[k, i * group + r])
            nums += [pv[:8, :HEAD], pv[8:, HEAD:]]
        num = jnp.concatenate(nums, axis=0) + own.astype(BF16).astype(F32) * vns[at, :]
        att[at, :] = num / den

    def attended(k, m):
        for n in range(HEADS):
            at = pl.ds(m * HALF_ROWS * HEADS + n, HALF_ROWS, stride=HEADS)
            agbuf[k, m, z, y, :, n * HEAD : (n + 1) * HEAD] = att[at, :].astype(BF16)

    def gather_rings(k, m):
        low, high = slice(0, QCOLS // 2), slice(QCOLS // 2, QCOLS)
        first = [
            DirectGather(y, at_y, lambda j: agbuf.at[k, m, z, j, :, low]),
            DirectGather(z, at_z, lambda j: agbuf.at[k, m, j, y, :, high]),
        ]
        second = [
            RingGather(
                z, at_z, lambda j, hf: agbuf.at[k, m, j, 2 * hf : 2 * hf + 2, :, low]
            ),
            RingGather(
                y, at_y, lambda j, hf: agbuf.at[k, m, 2 * hf : 2 * hf + 2, j, :, high]
            ),
        ]
        return first, second

    def gather_begin(k, m):
        for r in gathers[k][m][0]:
            r.begin()

    def gather_second(k, m):
        first, second = gathers[k][m]
        for n in range(2):
            first[n].end()
            second[n].begin()

    def gather_middle(k, m):
        for r in gathers[k][m][1]:
            r.middle()

    def gather_end(k, m):
        for r in gathers[k][m][1]:
            r.end()

    def down_product(k, m):
        rows = agbuf[k, m].reshape(256, QCOLS)
        down = dot(rows, wo[:, FEAT:]).T
        ids = half_slot[k, m, 0:1, :]
        acc = jnp.zeros((RANK, 256), F32)
        for n in range(16):
            slot = ((s if n < 8 else o) * 16 + p) * 8 + n % 8
            acc = acc + jnp.where(ids == slot, down[n * RANK : (n + 1) * RANK, :], 0.0)
        pad = jnp.zeros((RANK, 64), F32)
        for j in range(RING):
            lrown[k, m, j] = jnp.concatenate([acc[:, j * 64 : (j + 1) * 64], pad], axis=1)
        for c in lows[k][m]:
            c.start()

    def out_product(k, m):
        rows = agbuf[k, m].reshape(256, QCOLS)
        ob[k, m] = dot(rows, wo[:, :FEAT]).astype(BF16).reshape(4, 4, HALF_ROWS, FEAT)
        for d in (2, 1, 3):
            tops[k][m][d - 1].start()

    def low_copy(k, m, d):
        return pltpu.make_async_remote_copy(
            src_ref=lrp.at[k, m, p],
            dst_ref=lrp.at[k, m, p],
            send_sem=psend.at[k, m, d],
            recv_sem=precv.at[k, m, d],
            device_id={"pool": lax.rem(p + d, 16)},
            device_id_type=MESH,
        )

    def output_low(k, m):
        total = lrown[k, m, t]
        for d in range(1, RING):
            lows[k][m][d - 1].wait_recv()
            total = total + lrx[k, m, ring(t, -d)]
        lrp[k, m, p] = total.astype(BF16)

        def give(d, _):
            low_copy(k, m, d).start()
            return _

        lax.fori_loop(1, 16, give, 0)

    def output_delta(k, m):
        def receive(d, _):
            low_copy(k, m, d).wait()
            return _

        lax.fori_loop(1, 16, receive, 0)
        low_rank = lrp[k, m, 0].astype(F32)
        for n in range(1, 16):
            low_rank = low_rank + lrp[k, m, n].astype(F32)
        if m == 0:
            for c in panels[k]:
                c.wait_recv()
        block = lax.shift_right_logical(chunk_slot[k, m, t, 0:1, :], 3)
        wide = jnp.concatenate(
            [jnp.where(block == b, low_rank, 0.0) for b in range(32)], axis=0
        )
        delta = dot(wide.T[:64].astype(BF16), upbuf[k].reshape(512, FEAT))
        total = xin[k, m, t].astype(F32) + ob[k, m, t].astype(F32)
        for c in tops[k][m]:
            c.wait_recv()
        for d in range(3):
            total = total + finx[k, m, d].astype(F32)
        outs[k][0, :, m] = (
            total + ADAPTER_SCALE * delta.reshape(RING, HALF_ROWS, FEAT)
        ).astype(BF16)

    def slots_and_offsets():
        ids = [aor_ref[pl.ds(s + 1 - k, 1), :] for k in range(2)]
        first_block = (s * RING + t) * 4

        def step(a, carry):
            rows, offs = carry
            slots = [table_ref[apb_ref[c, a]] for c in range(3)]
            new_offs = []
            for c in range(3):
                block = lax.shift_right_logical(slots[c], 3) - first_block
                new_offs += [
                    jnp.where(block == j, slots[c] & 7, offs[4 * c + j]) for j in range(4)
                ]
            new_rows = []
            for k in range(2):
                slot = jnp.where(s == 0, slots[1 - k], slots[2 - k])
                new_rows.append(jnp.where(ids[k] == a, slot, rows[k]))
            return tuple(new_rows), tuple(new_offs)

        rows, offs = lax.fori_loop(
            0,
            32,
            step,
            ((jnp.zeros((1, ROWS), jnp.int32),) * 2, (jnp.int32(0),) * 12),
        )
        for k in range(2):

            def piece(j, b, m):
                at = (j * RING + b) * OWN_ROWS + m * HALF_ROWS
                return rows[k][:, at : at + HALF_ROWS]

            for m in range(2):
                half_slot[k, m, 0:1, :] = jnp.concatenate(
                    [piece(j, b, m) for j in range(RING) for b in range(RING)], axis=1
                )
                for j in range(RING):
                    part = jnp.concatenate([piece(j, b, m) for b in range(RING)], axis=1)
                    chunk_slot[k, m, j, 0:1, :] = jnp.concatenate([part, part], axis=1)
        return offs

    panels = [[], []]
    holder = s * RING + t
    for w in range(2):
        for k in range(2):
            for d in range(1 if w == 0 else 0, RING):
                panels[k].append(
                    tracked(
                        sel.at[w, k],
                        upbuf.at[k, holder],
                        {"section": s if w == 0 else o, "tensor": ring(t, d)},
                    )
                )

    def give_panels(offs):
        load_up.wait()
        for w in range(2):
            layer = s if w == 0 else o
            for k in range(2):
                for j in range(4):
                    off = jnp.where(layer == 0, offs[4 * (1 - k) + j], offs[4 * (2 - k) + j])
                    sel[w, k, j * RANK : (j + 1) * RANK, :] = upv[8 * j + off, layer]
                if w == 0:
                    upbuf[k, holder] = sel[w, k]
        for k in range(2):
            for c in panels[k]:
                c.start()

    def spread_down():
        for n in range(2):
            for m in range(QCOLS // 128):
                panel = dn[n, :, :, m * 128 : (m + 1) * 128].reshape(8 * RANK, 128)
                wo[m * 128 : (m + 1) * 128, FEAT + n * 128 : FEAT + (n + 1) * 128] = (
                    panel.astype(F32).T.astype(BF16)
                )

    rings = [[pool_rings(k, m) for m in range(2)] for k in range(2)]
    gathers = [[gather_rings(k, m) for m in range(2)] for k in range(2)]
    lows = [
        [
            [
                tracked(lrown.at[k, m, ring(t, d)], lrx.at[k, m, t], at_x(ring(t, d)))
                for d in range(1, RING)
            ]
            for m in range(2)
        ]
        for k in range(2)
    ]
    tops = [
        [
            [
                tracked(ob.at[k, m, ring(t, d)], finx.at[k, m, d - 1], at_x(ring(t, d)))
                for d in range(1, RING)
            ]
            for m in range(2)
        ]
        for k in range(2)
    ]

    def drain(copies):
        for c in copies:
            c.wait_send()
            started[:] = [other for other in started if other is not c]

    def ring_copies(which):
        return [
            c
            for m in range(2)
            for stage in which[m]
            for r in stage
            for c in r.copies
        ]

    for c in load_x0:
        c.wait()
    load_wq.wait()
    load_up.start()
    load_c[0].start()

    @pl.when(s == 0)
    def _():
        for c in load_fresh:
            c.start()

    load_wo.start()
    load_dn.start()
    load_c[1].start()
    other_down = tracked(down_hbm.at[:, o], dn.at[1], {"section": o})

    def everyone_is_here():
        pl.semaphore_wait(barrier, 22)

    @pl.when(s == 0)
    def _():
        project(0, 0, begin=True, ready=everyone_is_here)
        other_down.start()
        project(0, 1)
        sum_middle(0, 0)
        sum_begin(0, 1)
        pl.semaphore_signal(turn, inc=1, device_id={"section": o}, device_id_type=MESH)
        offs = slots_and_offsets()
        sum_middle(0, 1)
        sum_second(0, 0)
        give_panels(offs)
        for c in load_fresh:
            c.wait()
        project(1, 0)

    @pl.when(s == 1)
    def _():
        project(0, 0)
        everyone_is_here()
        other_down.start()
        project(0, 1)
        give_panels(slots_and_offsets())
        pl.semaphore_wait(turn, 1)
        sum_begin(0, 0)
        sum_middle(0, 0)
        sum_begin(0, 1)
        sum_middle(0, 1)
        sum_second(0, 0)

    sum_end(0, 0)
    sum_second(0, 1)

    load_c[0].wait()
    attention(0, 0)
    attention(0, 1)
    attended(0, 0)
    gather_begin(0, 0)
    sum_end(0, 1)
    attention(0, 2)
    gather_second(0, 0)
    attention(0, 3)
    attended(0, 1)
    gather_begin(0, 1)
    gather_middle(0, 0)
    gather_second(0, 1)
    load_dn.wait()
    other_down.wait_recv()
    load_wo.wait()
    spread_down()
    gather_end(0, 0)
    gather_middle(0, 1)

    @pl.when(s == 0)
    def _():
        sum_begin(1, 0)
        project(1, 1)

    down_product(0, 0)
    out_product(0, 0)

    relay = [
        [
            remote(
                first_ref.at[0, :, m], xin.at[1, m, t], {"section": 1, "tensor": ring(t, d)}
            )
            for d in range(RING)
        ]
        for m in range(2)
    ]

    def relay_start(m):
        for d in (2, 1, 3, 0):
            relay[m][d].start()

    def relay_wait(m):
        for c in relay[m]:
            c.wait_recv()

    @pl.when(s == 0)
    def _():
        output_low(0, 0)
        gather_end(0, 1)
        down_product(0, 1)
        output_delta(0, 0)
        relay_start(0)
        sum_middle(1, 0)
        sum_begin(1, 1)
        out_product(0, 1)
        output_low(0, 1)
        sum_middle(1, 1)
        output_delta(0, 1)
        relay_start(1)
        sum_second(1, 0)
        for m in range(2):
            for c in relay[m]:
                c.wait_send()

    @pl.when(s == 1)
    def _():
        output_low(0, 0)
        gather_end(0, 1)
        relay_wait(0)
        project(1, 0, begin=True)
        down_product(0, 1)
        sum_middle(1, 0)
        relay_wait(1)
        project(1, 1)
        sum_begin(1, 1)
        sum_second(1, 0)
        out_product(0, 1)
        sum_middle(1, 1)
        output_low(0, 1)
        output_delta(0, 0)

    sum_end(1, 0)
    sum_second(1, 1)
    load_c[1].wait()
    attention(1, 0)
    attention(1, 1)
    attended(1, 0)
    gather_begin(1, 0)
    sum_end(1, 1)
    attention(1, 2)
    gather_second(1, 0)
    attention(1, 3)
    attended(1, 1)
    gather_begin(1, 1)
    gather_middle(1, 0)
    drain(ring_copies(rings[0]))
    gather_second(1, 1)

    @pl.when(s == 1)
    def _():
        output_delta(0, 1)

    gather_end(1, 0)
    gather_middle(1, 1)
    drain(ring_copies(gathers[0]))
    down_product(1, 0)
    out_product(1, 0)
    output_low(1, 0)
    drain([other_down] + lows[0][0] + lows[0][1] + panels[0] + panels[1])
    drain(tops[0][0] + tops[0][1])
    gather_end(1, 1)
    down_product(1, 1)
    out_product(1, 1)
    output_delta(1, 0)
    output_low(1, 1)
    drain(ring_copies(rings[1]))
    drain(ring_copies(gathers[1]))
    output_delta(1, 1)
    drain(list(started))


def hand_over(first_in, second_in, first_out, second_out):
    first_out[...] = first_in[...]
    second_out[...] = second_in[...]


def on_device(hidden_input, fresh, *args):
    rows = (RING, RING, 2, HALF_ROWS, FEAT)
    any_space = pl.BlockSpec(memory_space=pl.ANY)
    vmem = pl.BlockSpec(memory_space=pltpu.VMEM)
    smem = pl.BlockSpec(memory_space=pltpu.SMEM)
    out = jax.ShapeDtypeStruct((1, RING, 2, HALF_ROWS, FEAT), BF16)
    v = pltpu.VMEM
    dma = pltpu.SemaphoreType.DMA
    first, second = pl.pallas_call(
        kernel,
        out_shape=(out, out),
        in_specs=[
            any_space,
            any_space,
            vmem,
            any_space,
            any_space,
            any_space,
            any_space,
            smem,
            vmem,
            smem,
            smem,
            any_space,
            any_space,
        ],
        out_specs=(vmem, vmem),
        scratch_shapes=[
            v((FEAT, QCOLS + 2 * KVCOLS), BF16),
            v((2 * FEAT, KVCOLS), BF16),
            v((QCOLS, FEAT + 16 * RANK), BF16),
            v((2, 8, RANK, QCOLS), BF16),
            v((32, 2, RANK, FEAT), BF16),
            v((2, 2, 4 * RANK, FEAT), BF16),
            v((2, 8, 4 * RANK, FEAT), BF16),
            v((2, OWN_ROWS, 2 * CTX, KVCOLS), BF16),
            v((2, 2, RING, RING, HALF_ROWS, CW), BF16),
            v((2, 2, 2, 2, 2, HALF_ROWS, WIDTHS[0]), BF16),
            v((2, 2, 2, 2, RING, HALF_ROWS, WIDTHS[0]), BF16),
            v((2, 2, 2, RING, HALF_ROWS, WIDTHS[0]), BF16),
            v((2, 2, 2, 3, HALF_ROWS, WIDTHS[0]), BF16),
            v((2, 2, RING, RING, HALF_ROWS, QCOLS), BF16),
            v((2, 2, RING, RING, HALF_ROWS, FEAT), BF16),
            v((2, 2, 3, RING, HALF_ROWS, FEAT), BF16),
            v((2, 2, RING, RING, HALF_ROWS, FEAT), BF16),
            v((ROWS // 2, FEAT), BF16),
            v((2, 2, 8, 256), jnp.int32),
            v((2, 2, RING, 8, 128), jnp.int32),
            v((OWN_ROWS * HEADS, HEAD), F32),
            v((OWN_ROWS * HEADS, HEAD), F32),
            v((OWN_ROWS * HEADS, HEAD), F32),
            v((OWN_ROWS * HEADS, HEAD), F32),
            v((2, 2, RING, RANK, 128), F32),
            v((2, 2, RING, RANK, 128), F32),
            v((2, 2, 16, RANK, 128), BF16),
            dma((N_SEM,)),
            dma((N_SEM,)),
            dma((11,)),
            dma((2, 2, 16)),
            dma((2, 2, 16)),
            pltpu.SemaphoreType.REGULAR,
        ],
        compiler_params=pltpu.CompilerParams(
            collective_id=0, has_side_effects=True, vmem_limit_bytes=58 * 2**20
        ),
        cost_estimate=pl.CostEstimate(
            flops=8_000_000_000, bytes_accessed=16_000_000, transcendentals=500_000
        ),
    )(hidden_input.reshape(rows), fresh.reshape(rows), *args)
    first, second = pl.pallas_call(
        hand_over,
        out_shape=(out, out),
        in_specs=[vmem, vmem],
        out_specs=(vmem, vmem),
    )(first, second)
    return first.reshape(1, 128, FEAT), second.reshape(1, 128, FEAT)


def solution(mesh):
    return jax.shard_map(
        on_device,
        mesh=mesh,
        in_specs=(
            P("section", None, "pool"),
            P(None, "pool"),
            P("section", "pool"),
            P("section", "pool", "tensor"),
            P("section", "pool", None, "tensor"),
            P("section", "tensor", "pool"),
            P("section", None, "pool", None, None, "tensor"),
            P(),
            P(),
            P(),
            P(),
            P(("section", "pool"), None, None, "tensor"),
            P(("section", "tensor"), None, None, "pool"),
        ),
        out_specs=(P("section", "tensor", "pool"), P("section", "tensor", "pool")),
        check_vma=False,
    )
```
